256 devices in a mesh: ctx: 16 (over y, x), head: 16 (over z, core).
Axes of the slice: x: 4, y: 4, z: 8, core: 2. Of those that a mesh axis runs over, the one named last changes fastest.
Arguments:
- queries: bfloat16 [2048, 24576], P(('ctx', 'head')), may hold values from -400 to 400
- cache_latent: bfloat16 [1024, 64, 512], P('ctx'), may hold values from -6 to 6
- cache_rope: bfloat16 [1024, 4096], P('ctx'), may hold values from -6 to 6
- selected: int32 [32, 32], replicated, may hold values from 0 to 1023, as said below
- w_uk: bfloat16 [128, 128, 512], P('head'), may hold values from -0.5 to 0.5
- value_up_weight: bfloat16 [128, 512, 128], P('head'), may hold values from -0.25 to 0.25
Outputs:
- attended: bfloat16 [2048, 128, 128], P('ctx', 'head')
The draws below stay inside these ranges and needn't reach their ends.
Inputs may be any that keep to these rules, and one draw needn't show every extreme that they name: `selected`: in each row the 32 block numbers are distinct; at most 4 of them share the value of number // 64, and in every row some value is shared by exactly 4.
All inputs are finite; a program needn't handle non-finite values.
Results may differ from the reference program's by a relative error of at most 0.014.
Values may be sent and summed in bfloat16 or wider, within the bound.
A program may use at most 192 MiB of HBM per device.

```python
import math
import jax
import jax.numpy as jnp
from jax import lax

H = 128
NOPE = 128
ROPE = 64
KVL = 512
VHD = 128
BLK = 64
SEL = 32
CTX_DEV = 4096
ROWS = 2048
QB = 32
NBLK = 1024
N_CTX = 16


def rope_base(key):
    return jnp.clip(jax.random.normal(jax.random.fold_in(key, 21), (NBLK, BLK, ROPE), jnp.float32), -5.0, 5.0)


def choose_blocks(key):
    key = jax.random.fold_in(key, 33)
    per_shard = CTX_DEV // BLK
    shard_most = 2 * SEL // N_CTX
    slot_count = N_CTX * shard_most

    def one_row(row_key):
        key_full, key_shuffle, key_local, key_order = jax.random.split(row_key, 4)
        full_owner = jax.random.randint(key_full, (), 0, N_CTX)
        shuffled = jax.random.permutation(key_shuffle, slot_count)
        order_key = jnp.where(shuffled // shard_most == full_owner, 0, slot_count) + jnp.arange(slot_count)
        chosen = shuffled[jnp.argsort(order_key, stable=True)][:SEL]
        owner_id = chosen // shard_most
        local_orders = jax.vmap(lambda inner_key: jax.random.permutation(inner_key, per_shard))(jax.random.split(key_local, N_CTX))
        local_block = local_orders[owner_id, chosen % shard_most]
        return jax.random.permutation(key_order, owner_id * per_shard + local_block)
    return jax.vmap(one_row)(jax.random.split(key, QB)).astype(jnp.int32)


def draw_selected(key, part):
    return choose_blocks(key)


def draw_cache_rope(key, part):
    base_keys = rope_base(key)
    paired = base_keys
    return paired.reshape(NBLK, BLK * ROPE).astype(jnp.bfloat16)


def draw_queries(key, part):
    key = jax.random.fold_in(key, 9)
    value_rows = jax.random.normal(key, (ROWS, H, NOPE + ROPE), jnp.float32)
    return value_rows.reshape(ROWS, H * (NOPE + ROPE)).astype(jnp.bfloat16)


def levels(rng, extent, cuts, low, top_value):
    level, own = 1.0, jax.random.fold_in(rng, 6)
    for position, parts in cuts:
        steps = jnp.exp(jax.random.uniform(jax.random.fold_in(own, position), (parts,), jnp.float32, low / len(cuts), top_value / len(cuts)))
        level = level * jnp.repeat(steps, extent[position] // parts).reshape([-1 if axis == position else 1 for axis in range(len(extent))])
    return level


def gaussian(own_key, shape, scale, reach, cuts=(), kind=jnp.bfloat16):
    level = levels(own_key, shape, cuts, -0.22, 0.18) if cuts else 1.0
    drawn = jax.random.normal(own_key, shape, jnp.float32) * scale * level
    return jnp.minimum(jnp.maximum(drawn, -reach), reach).astype(kind)


def setup_inputs(seed: int = 0) -> dict:
    splits = jax.random.split(jax.random.key(seed), 7)
    return {
        "queries": draw_queries(jax.random.fold_in(splits[6], 71), 0),
        "cache_latent": gaussian(splits[1], (NBLK, BLK, KVL), 1.0, 6.0, ((0, 16),)),
        "cache_rope": draw_cache_rope(jax.random.fold_in(splits[6], 71), 0),
        "selected": draw_selected(jax.random.fold_in(splits[6], 71), 0),
        "w_uk": gaussian(splits[4], (H, NOPE, KVL), NOPE ** -0.5, 0.5, ((0, 16),)),
        "value_up_weight": gaussian(splits[5], (H, KVL, VHD), KVL ** -0.5, 0.25, ((0, 16),)),
    }


def reference(queries, cache_latent, cache_rope, selected, w_uk, value_up_weight):
    split_heads = queries.reshape(ROWS, H, NOPE + ROPE)
    latent_query = jnp.einsum('rhn,hnk->rhk', split_heads[:, :, :NOPE].astype(jnp.float32), w_uk.astype(jnp.float32))
    latent_query = lax.optimization_barrier(latent_query.astype(jnp.bfloat16)).astype(jnp.float32)
    rope_query = split_heads[:, :, NOPE:].astype(jnp.float32)
    score_scale = 1.0 / math.sqrt(NOPE + ROPE)
    value_weight_matrix = value_up_weight.astype(jnp.float32)

    def one_block(block_id):
        start = (block_id * BLK).astype(jnp.int32)
        block_latent = lax.dynamic_slice_in_dim(latent_query, start, BLK, 0)
        block_rope = lax.dynamic_slice_in_dim(rope_query, start, BLK, 0)
        picked = selected[block_id]
        latent_rows = cache_latent[picked].reshape(SEL * BLK, KVL).astype(jnp.float32)
        rope_rows = cache_rope[picked].reshape(SEL * BLK, ROPE).astype(jnp.float32)
        from_latent = jnp.einsum('rhk,tk->rht', block_latent, latent_rows)
        from_rope = jnp.einsum('rhe,te->rht', block_rope, rope_rows)
        scores = (from_latent + from_rope) * score_scale
        row_top = lax.optimization_barrier(jnp.max(scores, axis=2, keepdims=True))
        weights = jnp.exp(scores - row_top)
        row_total = lax.optimization_barrier(jnp.sum(weights, axis=2))
        weights_low = lax.optimization_barrier(weights.astype(jnp.bfloat16)).astype(jnp.float32)
        blended_latent_rows = jnp.einsum('rht,tk->rhk', weights_low, latent_rows)
        value_rows = jnp.einsum('diz,izw->diw', blended_latent_rows, value_weight_matrix, precision=lax.Precision.HIGHEST)
        return (value_rows / row_total[:, :, None]).astype(jnp.bfloat16)
    result = lax.map(one_block, jnp.arange(QB, dtype=jnp.int32))
    return result.reshape(ROWS, H, VHD)
```

```python
import functools
import math

import jax
import jax.numpy as jnp
from jax import lax
from jax.experimental import pallas as pl
from jax.experimental.pallas import tpu as pltpu
from jax.sharding import PartitionSpec as P

NOPE = 128
ROPE = 64
KVL = 512
VHD = 128
BLK = 64
HALF = KVL // 2
N_CTX = 16
N_HEAD = 16
HEADS = 8
HEAD_COLS = HEADS * (NOPE + ROPE)
SLOT = 144
CLASSES = 8
PICKS = 8
MESH = pl.DeviceIdType.MESH
DIRECT = (0, 4, 3)
RING_STEPS = 2
SUBS = 2
SUB = PICKS // SUBS
NT = (((1,), (1,)), ((), ()))
ROW_TILE = 256
SCALE = math.log2(math.e) / math.sqrt(NOPE + ROPE)


def kernel(
    q_hbm,
    cache_hbm,
    rope_hbm,
    sel_hbm,
    w_hbm,
    v_hbm,
    out,
    sel_v,
    rank_v,
    tab_v,
    tab,
    out_wide,
    cache_v,
    rope_land,
    rope_wide,
    rope_v,
    rope_keys,
    w_v,
    v_v,
    q_land,
    q_all,
    acc,
    top,
    total,
    g_mine,
    g_other,
    *rest,
):
    nd = len(DIRECT)
    send_bufs, recv_bufs = rest[:nd], rest[nd : 2 * nd]
    (
        local_sem,
        q_send,
        q_recv,
        xy_send,
        xy_recv,
        ring_send,
        ring_recv,
        last_send,
        last_recv,
        core_send,
        core_recv,
    ) = rest[2 * nd :]
    ctx = lax.axis_index("ctx")
    head = lax.axis_index("head")
    z = lax.div(head, 2)
    core = lax.rem(head, 2)

    def direct(d):
        return DIRECT[d] + 2 * core if d == 2 else DIRECT[d]

    def local_copies():
        mine = pl.multiple_of(core * HALF, HALF)
        other = pl.multiple_of(HALF - core * HALF, HALF)
        cols = pl.ds(pl.multiple_of(head * HEAD_COLS, 128), HEAD_COLS)
        return [
            pltpu.make_async_copy(
                cache_hbm.at[:, :, pl.ds(mine, HALF)], cache_v, local_sem.at[0]
            ),
            pltpu.make_async_copy(
                rope_hbm.at[:, pl.ds(pl.multiple_of(core * 2048, 2048), 2048)],
                rope_land,
                local_sem.at[1],
            ),
            pltpu.make_async_copy(q_hbm.at[:, cols], q_land.at[:, cols], local_sem.at[2]),
            pltpu.make_async_copy(
                w_hbm.at[:, :, pl.ds(mine, HALF)], w_v.at[:, :, pl.ds(0, HALF)], local_sem.at[3]
            ),
            pltpu.make_async_copy(
                w_hbm.at[:, :, pl.ds(other, HALF)],
                w_v.at[:, :, pl.ds(HALF, HALF)],
                local_sem.at[4],
            ),
            pltpu.make_async_copy(
                v_hbm.at[:, pl.ds(mine, HALF)], v_v.at[:, pl.ds(0, HALF)], local_sem.at[5]
            ),
            pltpu.make_async_copy(
                v_hbm.at[:, pl.ds(other, HALF)], v_v.at[:, pl.ds(HALF, HALF)], local_sem.at[6]
            ),
            pltpu.make_async_copy(sel_hbm, sel_v, local_sem.at[7]),
        ]

    copies = local_copies()
    for place in (7, 0, 1, 2, 3, 4, 5, 6):
        copies[place].start()

    barrier = pltpu.get_barrier_semaphore()

    @pl.loop(1, N_CTX)
    def _(i):
        pl.semaphore_signal(
            barrier,
            inc=1,
            device_id={"ctx": lax.rem(ctx + i, N_CTX), "head": head},
            device_id_type=MESH,
        )
        pl.semaphore_signal(
            barrier,
            inc=1,
            device_id={"ctx": ctx, "head": lax.rem(head + i, N_HEAD)},
            device_id_type=MESH,
        )

    copies[7].wait()
    sel = sel_v[...]
    rank = jnp.zeros_like(sel)
    for j in range(32):
        rank += (sel[:, j : j + 1] < sel).astype(jnp.int32)
    mine = lax.shift_right_logical(sel, 6) == ctx
    tab_v[...] = jnp.zeros_like(tab_v)
    for m in range(4):
        here = jnp.logical_and(mine, (rank & 3) == m)
        block = jnp.sum(jnp.where(here, sel & 63, 0), axis=1, keepdims=True)
        tab_v[0:32, m : m + 1] = block
    rank_v[...] = rank
    own_rank = rank_v[pl.ds(2 * ctx, 2), :]
    own_from = lax.shift_right_logical(sel_v[pl.ds(2 * ctx, 2), :], 6)
    position = lax.broadcasted_iota(jnp.int32, (2, 32), 1)
    source = jnp.zeros((2, 32), jnp.int32)
    for j in range(32):
        source += jnp.where(position == own_rank[:, j : j + 1], own_from[:, j : j + 1], 0)
    tab_v[32:34, 0:32] = source
    tab_copy = pltpu.make_async_copy(tab_v, tab, local_sem.at[8])
    tab_copy.start()

    def q_copy(i):
        to = lax.rem(head + i, N_HEAD)
        return pltpu.make_async_remote_copy(
            src_ref=q_hbm.at[:, pl.ds(pl.multiple_of(to * HEAD_COLS, 128), HEAD_COLS)],
            dst_ref=q_land.at[:, pl.ds(pl.multiple_of(head * HEAD_COLS, 128), HEAD_COLS)],
            send_sem=q_send.at[i],
            recv_sem=q_recv.at[i],
            device_id={"ctx": ctx, "head": to},
            device_id_type=MESH,
        )

    def xy_copy(d, i):
        return pltpu.make_async_remote_copy(
            src_ref=send_bufs[d].at[i],
            dst_ref=recv_bufs[d].at[ctx],
            send_sem=xy_send.at[d, i],
            recv_sem=xy_recv.at[d, i],
            device_id={"ctx": lax.rem(ctx + i, N_CTX), "head": head},
            device_id_type=MESH,
        )

    def picked(d, to):
        group = lax.rem(z + direct(d), CLASSES)
        block = tab[2 * to + lax.div(group, 4), lax.rem(group, 4)]
        return cache_v[block], rope_v[block]

    def stage(d):
        @pl.loop(1, N_CTX, unroll=5)
        def _(i):
            latent, rope = picked(d, lax.rem(ctx + i, N_CTX))
            send_bufs[d][i, 0:64, :] = latent[:, :128]
            send_bufs[d][i, 64:128, :] = latent[:, 128:]
            send_bufs[d][i, 128:144, :] = rope

        latent, rope = picked(d, ctx)
        recv_bufs[d][ctx, 0:64, :] = latent[:, :128]
        recv_bufs[d][ctx, 64:128, :] = latent[:, 128:]
        recv_bufs[d][ctx, 128:144, :] = rope

    def give(d):
        @pl.loop(1, N_CTX, unroll=5)
        def _(i):
            xy_copy(d, i).start()

    pl.semaphore_wait(barrier, 2 * (N_CTX - 1))

    @pl.loop(1, N_HEAD)
    def _(i):
        q_copy(i).start()

    copies[1].wait()
    for i in range(16):
        rope_wide[pl.ds(i, 64, stride=16), :] = rope_land[:, i * 128 : i * 128 + 128].astype(
            jnp.float32
        )
    rope_v[...] = rope_wide[...].astype(jnp.bfloat16).reshape(64, 16, 128)
    copies[0].wait()
    tab_copy.wait()
    stage(0)
    give(0)
    for d in range(1, nd):
        stage(d)

    acc[...] = jnp.zeros_like(acc)
    total[...] = jnp.zeros_like(total)
    top[...] = jnp.full_like(top, -1e30)

    def ring_copy(direction, step, sub):
        source = (CLASSES - step) % CLASSES if direction == 0 else step
        target = CLASSES - step - 1 if direction == 0 else step + 1
        to = lax.rem(head + (2 if direction == 0 else N_HEAD - 2), N_HEAD)
        part = pl.ds(sub * SUB, SUB)
        return pltpu.make_async_remote_copy(
            src_ref=g_mine.at[source, part],
            dst_ref=g_mine.at[target, part],
            send_sem=ring_send.at[direction, step, sub],
            recv_sem=ring_recv.at[direction, step, sub],
            device_id={"ctx": ctx, "head": to},
            device_id_type=MESH,
        )

    last = 5 - 2 * core

    def last_copy(sub):
        part = pl.ds(sub * SUB, SUB)
        return pltpu.make_async_remote_copy(
            src_ref=g_mine.at[6 - 4 * core, part],
            dst_ref=g_mine.at[last, part],
            send_sem=last_send.at[sub],
            recv_sem=last_recv.at[sub],
            device_id={"ctx": ctx, "head": lax.rem(head + 2 + (N_HEAD - 4) * core, N_HEAD)},
            device_id_type=MESH,
        )

    def core_copy(rel, sub):
        part = pl.ds(sub * SUB, SUB)
        return pltpu.make_async_remote_copy(
            src_ref=g_mine.at[rel, part],
            dst_ref=g_other.at[rel, part],
            send_sem=core_send.at[rel, sub],
            recv_sem=core_recv.at[rel, sub],
            device_id={"ctx": ctx, "head": head + 1 - 2 * core},
            device_id_type=MESH,
        )

    def share(rel):
        for sub in range(SUBS):
            core_copy(rel, sub).start()

    def take(d):
        @pl.loop(1, 12)
        def _(i):
            xy_copy(d, i).wait_recv()

        if d == 0:
            give(1)

        @pl.loop(12, N_CTX)
        def _(i):
            xy_copy(d, i).wait_recv()

        rel = direct(d)
        group = lax.rem(z + rel, CLASSES)
        row = 32 + lax.div(group, 4)
        for j in range(PICKS):
            g_mine[rel, j] = recv_bufs[d][tab[row, lax.rem(group, 4) + 4 * j]]

    def load(rel, first, count, place):
        picks = pl.ds(first, count)
        latent = jnp.concatenate(
            [
                g_mine[rel, picks, 0:64, :],
                g_mine[rel, picks, 64:128, :],
                g_other[rel, picks, 0:64, :],
                g_other[rel, picks, 64:128, :],
            ],
            axis=2,
        ).reshape(count * BLK, KVL)
        lane_low = lax.broadcasted_iota(jnp.int32, (count, 16, 128), 2) < 64
        for held, half in ((g_mine, core), (g_other, 1 - core)):
            pairs = held[rel, picks, 128:144, :].astype(jnp.float32)
            zero = jnp.zeros_like(pairs)
            even = pl.ds(32 * half, 16, stride=2)
            odd = pl.ds(32 * half + 1, 16, stride=2)
            rope_keys[place, 0:count, even, :] = jnp.where(lane_low, pairs, zero)
            rope_keys[place, 0:count, odd, :] = jnp.where(lane_low, zero, pairs)
        rope = rope_keys[place, 0:count].astype(jnp.bfloat16).reshape(count * BLK, 128)
        return latent, jnp.concatenate([latent, rope], axis=1)

    def attend(*items):
        for rel, first, count in items:
            for sub in range(first // SUB, (first + count) // SUB):
                core_copy(rel, sub).wait_recv()
        units = []
        for place, (rel, first, count) in enumerate(items):
            b = lax.div(lax.rem(z + rel, CLASSES), 4)
            latent, keys = load(rel, first, count, place)
            for tile in range(512 // ROW_TILE):
                units.append((b, pl.ds(tile * ROW_TILE, ROW_TILE), latent, keys))

        def score_unit(b, rows, _, keys):
            return lax.dot_general(q_all[b, rows, :], keys, NT, preferred_element_type=jnp.float32)

        score = score_unit(*units[0])
        for place, (b, rows, latent, keys) in enumerate(units):
            later = score_unit(*units[place + 1]) if place + 1 < len(units) else None
            before = top[b, rows, :]
            now = jnp.maximum(before, jnp.max(score, axis=1, keepdims=True))
            fade = jnp.exp2((before - now) * SCALE)
            parts = [
                jnp.exp2((score[:, c * 128 : c * 128 + 128] - now) * SCALE)
                for c in range(score.shape[1] // 128)
            ]
            top[b, rows, :] = now
            total[b, rows, :] = total[b, rows, :] * fade + sum(parts[1:], parts[0])
            weights = jnp.concatenate(parts, axis=1).astype(jnp.bfloat16)
            mixed = jnp.dot(weights, latent, preferred_element_type=jnp.float32)
            for c in range(4):
                cols = slice(c * 128, c * 128 + 128)
                acc[b, rows, cols] = acc[b, rows, cols] * fade + mixed[:, cols]
            score = later

    def forward(step, sub):
        for direction in range(2):
            ring_copy(direction, step, sub).wait_recv()
            if step + 1 < RING_STEPS:
                ring_copy(direction, step + 1, sub).start()
        if step + 1 == RING_STEPS:
            last_copy(sub).start()
        for rel in (CLASSES - step - 1, step + 1):
            core_copy(rel, sub).start()

    def end(sub):
        last_copy(sub).wait_recv()
        core_copy(last, sub).start()

    def absorb():
        copies[2].wait()

        @pl.loop(1, N_HEAD)
        def _(i):
            q_copy(i).wait_recv()

        copies[3].wait()
        copies[4].wait()
        low = lax.broadcasted_iota(jnp.int32, (8 * N_HEAD, 128), 1) < 64
        for pair in range(HEADS // 2):
            tiles = []
            for t in range(3):
                column = pair * 384 + t * 128
                tiles.append(
                    jnp.concatenate(
                        [
                            q_land[:, h * HEAD_COLS + column : h * HEAD_COLS + column + 128].astype(
                                jnp.float32
                            )
                            for h in range(N_HEAD)
                        ],
                        axis=0,
                    )
                )
            swap1 = pltpu.roll(tiles[1], 64, 1)
            swap2 = pltpu.roll(tiles[2], 64, 1)
            nopes = (tiles[0], jnp.where(low, swap1, swap2))
            ropes = (jnp.where(low, tiles[1], swap1), jnp.where(low, swap2, tiles[2]))
            for parity in range(2):
                n = 2 * pair + parity
                absorbed = jnp.dot(
                    nopes[parity].astype(jnp.bfloat16), w_v[n], preferred_element_type=jnp.float32
                ).astype(jnp.bfloat16)
                rope = ropes[parity].astype(jnp.bfloat16)
                for b in range(2):
                    q_all[b, n * 64 : n * 64 + 64, 0:KVL] = absorbed[b * 64 : b * 64 + 64]
                    q_all[b, n * 64 : n * 64 + 64, KVL:] = rope[b * 64 : b * 64 + 64]

    take(0)
    for sub in range(SUBS):
        for direction in range(2):
            ring_copy(direction, 0, sub).start()
    share(0)
    give(2)
    absorb()
    attend((0, 0, PICKS))
    forward(0, 0)
    attend((7, 0, SUB), (1, 0, SUB))
    forward(0, 1)
    take(1)
    share(4)
    attend((7, SUB, SUB), (1, SUB, SUB))
    forward(1, 0)
    attend((4, 0, PICKS), (6, 0, SUB), (2, 0, SUB))
    forward(1, 1)
    take(2)
    share(direct(2))
    attend((6, SUB, SUB), (2, SUB, SUB))
    end(0)
    attend((direct(2), 0, SUB), (last, 0, SUB))
    end(1)
    attend((direct(2), SUB, SUB), (last, SUB, SUB))

    copies[5].wait()
    copies[6].wait()
    for n in range(HEADS):
        rows = slice(n * 64, n * 64 + 64)
        mixed = acc[:, rows, :].reshape(128, KVL).astype(jnp.bfloat16)
        value = jnp.dot(mixed, v_v[n], preferred_element_type=jnp.float32)
        sums = jnp.sum(total[:, rows, :].reshape(128, 128), axis=1, keepdims=True)
        out_wide[pl.ds(n, 128, stride=HEADS), :] = value / sums
    out[...] = out_wide[...].astype(jnp.bfloat16).reshape(128, HEADS, VHD)

    @pl.loop(1, N_HEAD)
    def _(i):
        q_copy(i).wait_send()
        for d in range(nd):
            xy_copy(d, i).wait_send()

    for step in range(RING_STEPS):
        for sub in range(SUBS):
            for direction in range(2):
                ring_copy(direction, step, sub).wait_send()
    for sub in range(SUBS):
        last_copy(sub).wait_send()
        for rel in range(CLASSES):
            core_copy(rel, sub).wait_send()


def local(queries, cache_latent, cache_rope, selected, w_uk, value_up_weight):
    bf16 = jnp.bfloat16
    nd = len(DIRECT)
    dma = pltpu.SemaphoreType.DMA
    any_spec = pl.BlockSpec(memory_space=pl.ANY)
    return pl.pallas_call(
        kernel,
        out_shape=pltpu.VMEM((128, HEADS, VHD), bf16),
        in_specs=[any_spec] * 6,
        out_specs=pl.BlockSpec(memory_space=pltpu.VMEM),
        scratch_shapes=[
            pltpu.VMEM((32, 32), jnp.int32),
            pltpu.VMEM((32, 32), jnp.int32),
            pltpu.VMEM((40, 128), jnp.int32),
            pltpu.SMEM((40, 128), jnp.int32),
            pltpu.VMEM((128 * HEADS, VHD), jnp.float32),
            pltpu.VMEM((64, BLK, HALF), bf16),
            pltpu.VMEM((64, 2048), bf16),
            pltpu.VMEM((1024, 128), jnp.float32),
            pltpu.VMEM((64, 16, 128), bf16),
            pltpu.VMEM((3, PICKS, BLK, 128), jnp.float32),
            pltpu.VMEM((HEADS, NOPE, KVL), bf16),
            pltpu.VMEM((HEADS, KVL, VHD), bf16),
            pltpu.VMEM((8, N_HEAD * HEAD_COLS), bf16),
            pltpu.VMEM((2, 512, KVL + 128), bf16),
            pltpu.VMEM((2, 512, KVL), jnp.float32),
            pltpu.VMEM((2, 512, 128), jnp.float32),
            pltpu.VMEM((2, 512, 128), jnp.float32),
            pltpu.VMEM((CLASSES, PICKS, SLOT, 128), bf16),
            pltpu.VMEM((CLASSES, PICKS, SLOT, 128), bf16),
        ]
        + [pltpu.VMEM((N_CTX, SLOT, 128), bf16)] * (2 * nd)
        + [
            dma((9,)),
            dma((N_HEAD,)),
            dma((N_HEAD,)),
            dma((nd, N_CTX)),
            dma((nd, N_CTX)),
            dma((2, RING_STEPS, SUBS)),
            dma((2, RING_STEPS, SUBS)),
            dma((SUBS,)),
            dma((SUBS,)),
            dma((CLASSES, SUBS)),
            dma((CLASSES, SUBS)),
        ],
        compiler_params=pltpu.CompilerParams(
            collective_id=0, has_side_effects=True, vmem_limit_bytes=62 * 1024 * 1024
        ),
    )(queries, cache_latent, cache_rope, selected, w_uk, value_up_weight)


def solution(mesh):
    placed = (
        P(("ctx", "head"), None),
        P("ctx", None, None),
        P("ctx", None),
        P(),
        P("head", None, None),
        P("head", None, None),
    )
    return jax.shard_map(
        local, mesh=mesh, in_specs=placed, out_specs=P("ctx", "head", None), check_vma=False
    )
```

```python
import functools
import math

import jax
import jax.numpy as jnp
from jax import lax
from jax.experimental import pallas as pl
from jax.experimental.pallas import tpu as pltpu
from jax.sharding import PartitionSpec as P

NOPE = 128
ROPE = 64
KVL = 512
VHD = 128
BLK = 64
HALF = KVL // 2
N_CTX = 16
N_HEAD = 16
HEADS = 8
HEAD_COLS = HEADS * (NOPE + ROPE)
SLOT = 144
CLASSES = 8
PICKS = 8
MESH = pl.DeviceIdType.MESH
DIRECT = (0, 4, 3)
RING_STEPS = 2
SUBS = 2
SUB = PICKS // SUBS
SCALE = math.log2(math.e) / math.sqrt(NOPE + ROPE)


def kernel(*refs):
    spaces = [pltpu.ACC(t)((256, 256), jnp.float32) for t in (0, 0, 1, 1)] * 2
    pl.run_scoped(lambda *accumulators: body(accumulators, *refs), *spaces)


def body(
    accumulators,
    q_hbm,
    cache_hbm,
    rope_hbm,
    sel_hbm,
    w_hbm,
    v_hbm,
    out,
    sel_v,
    rank_v,
    tab_v,
    tab,
    out_wide,
    cache_v,
    rope_land,
    rope_wide,
    rope_v,
    rope_keys,
    w_v,
    v_v,
    q_land,
    q_all,
    acc,
    top,
    total,
    g_mine,
    g_other,
    *rest,
):
    nd = len(DIRECT)
    score_acc, mix_acc = accumulators[:4], accumulators[4:]
    send_bufs, recv_bufs = rest[:nd], rest[nd : 2 * nd]
    (
        local_sem,
        q_send,
        q_recv,
        xy_send,
        xy_recv,
        ring_send,
        ring_recv,
        last_send,
        last_recv,
        core_send,
        core_recv,
    ) = rest[2 * nd :]
    ctx = lax.axis_index("ctx")
    head = lax.axis_index("head")
    z = lax.div(head, 2)
    core = lax.rem(head, 2)

    def direct(d):
        return DIRECT[d] + 2 * core if d == 2 else DIRECT[d]

    def local_copies():
        mine = pl.multiple_of(core * HALF, HALF)
        other = pl.multiple_of(HALF - core * HALF, HALF)
        cols = pl.ds(pl.multiple_of(head * HEAD_COLS, 128), HEAD_COLS)
        return [
            pltpu.make_async_copy(
                cache_hbm.at[:, :, pl.ds(mine, HALF)], cache_v, local_sem.at[0]
            ),
            pltpu.make_async_copy(
                rope_hbm.at[:, pl.ds(pl.multiple_of(core * 2048, 2048), 2048)],
                rope_land,
                local_sem.at[1],
            ),
            pltpu.make_async_copy(q_hbm.at[:, cols], q_land.at[:, cols], local_sem.at[2]),
            pltpu.make_async_copy(
                w_hbm.at[:, :, pl.ds(mine, HALF)], w_v.at[:, :, pl.ds(0, HALF)], local_sem.at[3]
            ),
            pltpu.make_async_copy(
                w_hbm.at[:, :, pl.ds(other, HALF)],
                w_v.at[:, :, pl.ds(HALF, HALF)],
                local_sem.at[4],
            ),
            pltpu.make_async_copy(
                v_hbm.at[:, pl.ds(mine, HALF)], v_v.at[:, pl.ds(0, HALF)], local_sem.at[5]
            ),
            pltpu.make_async_copy(
                v_hbm.at[:, pl.ds(other, HALF)], v_v.at[:, pl.ds(HALF, HALF)], local_sem.at[6]
            ),
            pltpu.make_async_copy(sel_hbm, sel_v, local_sem.at[7]),
        ]

    copies = local_copies()
    for place in (7, 0, 1, 2, 3, 4, 5, 6):
        copies[place].start()

    barrier = pltpu.get_barrier_semaphore()

    @pl.loop(1, N_CTX)
    def _(i):
        pl.semaphore_signal(
            barrier,
            inc=1,
            device_id={"ctx": lax.rem(ctx + i, N_CTX), "head": head},
            device_id_type=MESH,
        )
        pl.semaphore_signal(
            barrier,
            inc=1,
            device_id={"ctx": ctx, "head": lax.rem(head + i, N_HEAD)},
            device_id_type=MESH,
        )

    copies[7].wait()
    sel = sel_v[...]
    rank = jnp.zeros_like(sel)
    for j in range(32):
        rank += (sel[:, j : j + 1] < sel).astype(jnp.int32)
    mine = lax.shift_right_logical(sel, 6) == ctx
    tab_v[...] = jnp.zeros_like(tab_v)
    for m in range(4):
        here = jnp.logical_and(mine, (rank & 3) == m)
        block = jnp.sum(jnp.where(here, sel & 63, 0), axis=1, keepdims=True)
        tab_v[0:32, m : m + 1] = block
    rank_v[...] = rank
    own_rank = rank_v[pl.ds(2 * ctx, 2), :]
    own_from = lax.shift_right_logical(sel_v[pl.ds(2 * ctx, 2), :], 6)
    position = lax.broadcasted_iota(jnp.int32, (2, 32), 1)
    source = jnp.zeros((2, 32), jnp.int32)
    for j in range(32):
        source += jnp.where(position == own_rank[:, j : j + 1], own_from[:, j : j + 1], 0)
    tab_v[32:34, 0:32] = source
    tab_copy = pltpu.make_async_copy(tab_v, tab, local_sem.at[8])
    tab_copy.start()

    def q_copy(i):
        to = lax.rem(head + i, N_HEAD)
        return pltpu.make_async_remote_copy(
            src_ref=q_hbm.at[:, pl.ds(pl.multiple_of(to * HEAD_COLS, 128), HEAD_COLS)],
            dst_ref=q_land.at[:, pl.ds(pl.multiple_of(head * HEAD_COLS, 128), HEAD_COLS)],
            send_sem=q_send.at[i],
            recv_sem=q_recv.at[i],
            device_id={"ctx": ctx, "head": to},
            device_id_type=MESH,
        )

    def xy_copy(d, i):
        return pltpu.make_async_remote_copy(
            src_ref=send_bufs[d].at[i],
            dst_ref=recv_bufs[d].at[ctx],
            send_sem=xy_send.at[d, i],
            recv_sem=xy_recv.at[d, i],
            device_id={"ctx": lax.rem(ctx + i, N_CTX), "head": head},
            device_id_type=MESH,
        )

    def picked(d, to):
        group = lax.rem(z + direct(d), CLASSES)
        block = tab[2 * to + lax.div(group, 4), lax.rem(group, 4)]
        return cache_v[block], rope_v[block]

    def stage(d):
        @pl.loop(1, N_CTX, unroll=5)
        def _(i):
            latent, rope = picked(d, lax.rem(ctx + i, N_CTX))
            send_bufs[d][i, 0:64, :] = latent[:, :128]
            send_bufs[d][i, 64:128, :] = latent[:, 128:]
            send_bufs[d][i, 128:144, :] = rope

        latent, rope = picked(d, ctx)
        recv_bufs[d][ctx, 0:64, :] = latent[:, :128]
        recv_bufs[d][ctx, 64:128, :] = latent[:, 128:]
        recv_bufs[d][ctx, 128:144, :] = rope

    def give(d):
        @pl.loop(1, N_CTX, unroll=5)
        def _(i):
            xy_copy(d, i).start()

    pl.semaphore_wait(barrier, 2 * (N_CTX - 1))

    @pl.loop(1, N_HEAD)
    def _(i):
        q_copy(i).start()

    copies[1].wait()
    for i in range(16):
        rope_wide[pl.ds(i, 64, stride=16), :] = rope_land[:, i * 128 : i * 128 + 128].astype(
            jnp.float32
        )
    rope_v[...] = rope_wide[...].astype(jnp.bfloat16).reshape(64, 16, 128)
    copies[0].wait()
    tab_copy.wait()
    stage(0)
    give(0)
    for d in range(1, nd):
        stage(d)

    acc[...] = jnp.zeros_like(acc)
    total[...] = jnp.zeros_like(total)
    top[...] = jnp.full_like(top, -1e30)
    q_all[:, :, KVL + 128 :] = jnp.zeros((2, 512, 128), jnp.bfloat16)

    def ring_copy(direction, step, sub):
        source = (CLASSES - step) % CLASSES if direction == 0 else step
        target = CLASSES - step - 1 if direction == 0 else step + 1
        to = lax.rem(head + (2 if direction == 0 else N_HEAD - 2), N_HEAD)
        part = pl.ds(sub * SUB, SUB)
        return pltpu.make_async_remote_copy(
            src_ref=g_mine.at[source, part],
            dst_ref=g_mine.at[target, part],
            send_sem=ring_send.at[direction, step, sub],
            recv_sem=ring_recv.at[direction, step, sub],
            device_id={"ctx": ctx, "head": to},
            device_id_type=MESH,
        )

    last = 5 - 2 * core

    def last_copy(sub):
        part = pl.ds(sub * SUB, SUB)
        return pltpu.make_async_remote_copy(
            src_ref=g_mine.at[6 - 4 * core, part],
            dst_ref=g_mine.at[last, part],
            send_sem=last_send.at[sub],
            recv_sem=last_recv.at[sub],
            device_id={"ctx": ctx, "head": lax.rem(head + 2 + (N_HEAD - 4) * core, N_HEAD)},
            device_id_type=MESH,
        )

    def core_copy(rel, sub):
        part = pl.ds(sub * SUB, SUB)
        return pltpu.make_async_remote_copy(
            src_ref=g_mine.at[rel, part],
            dst_ref=g_other.at[rel, part],
            send_sem=core_send.at[rel, sub],
            recv_sem=core_recv.at[rel, sub],
            device_id={"ctx": ctx, "head": head + 1 - 2 * core},
            device_id_type=MESH,
        )

    def share(rel):
        for sub in range(SUBS):
            core_copy(rel, sub).start()

    def take(d):
        @pl.loop(1, 12)
        def _(i):
            xy_copy(d, i).wait_recv()

        if d == 0:
            give(1)

        @pl.loop(12, N_CTX)
        def _(i):
            xy_copy(d, i).wait_recv()

        rel = direct(d)
        group = lax.rem(z + rel, CLASSES)
        row = 32 + lax.div(group, 4)
        for j in range(PICKS):
            g_mine[rel, j] = recv_bufs[d][tab[row, lax.rem(group, 4) + 4 * j]]

    lane_low = lax.broadcasted_iota(jnp.int32, (SUB, 16, 128), 2) < 64
    blank = jnp.zeros((SUB * BLK, 128), jnp.bfloat16)

    def load(rel, sub, place):
        picks = pl.ds(sub * SUB, SUB)
        found = []
        for held, half in ((g_mine, core), (g_other, 1 - core)):
            found.append(
                jnp.concatenate(
                    [held[rel, picks, 0:64, :], held[rel, picks, 64:128, :]], axis=2
                ).reshape(SUB * BLK, HALF)
            )
            pairs = held[rel, picks, 128:144, :].astype(jnp.float32)
            zero = jnp.zeros_like(pairs)
            even = pl.ds(32 * half, 16, stride=2)
            odd = pl.ds(32 * half + 1, 16, stride=2)
            rope_keys[place, :, even, :] = jnp.where(lane_low, pairs, zero)
            rope_keys[place, :, odd, :] = jnp.where(lane_low, zero, pairs)
        rope = rope_keys[place].astype(jnp.bfloat16).reshape(SUB * BLK, 128)
        found.append(jnp.concatenate([rope, blank], axis=1))
        return found

    def attend(*items):
        for rel, sub in items:
            core_copy(rel, sub).wait_recv()
        groups = [lax.div(lax.rem(z + rel, CLASSES), 4) for rel, _ in items]
        loaded = [load(rel, sub, place) for place, (rel, sub) in enumerate(items)]

        def score(place):
            for k in range(3):
                for t in range(2):
                    pltpu.matmul_push_rhs(loaded[place][k], k % 2, t, transpose=True)
                    pltpu.matmul_acc_lhs(
                        score_acc[2 * t + place % 2],
                        q_all[groups[place], t * 256 : t * 256 + 256, k * 256 : k * 256 + 256],
                        load_staged_rhs=k % 2,
                    )

        score(0)
        for place, b in enumerate(groups):
            if place + 1 < len(items):
                score(place + 1)
            fades = []
            for t in range(2):
                rows = slice(t * 256, t * 256 + 256)
                scores = pltpu.matmul_pop(score_acc[2 * t + place % 2])
                before = top[b, rows, :]
                now = jnp.maximum(before, jnp.max(scores, axis=1, keepdims=True))
                fade = jnp.exp2((before - now) * SCALE)
                parts = [
                    jnp.exp2((scores[:, c * 128 : c * 128 + 128] - now) * SCALE) for c in range(2)
                ]
                top[b, rows, :] = now
                total[b, rows, :] = total[b, rows, :] * fade + (parts[0] + parts[1])
                weights = jnp.concatenate(parts, axis=1).astype(jnp.bfloat16)
                fades.append(fade)
                for n in range(2):
                    pltpu.matmul_push_rhs(loaded[place][n], n, t)
                    pltpu.matmul_acc_lhs(mix_acc[2 * t + n], weights, load_staged_rhs=n)
            for t in range(2):
                rows = slice(t * 256, t * 256 + 256)
                for n in range(2):
                    mixed = pltpu.matmul_pop(mix_acc[2 * t + n])
                    for c in range(2):
                        cols = slice(n * 256 + c * 128, n * 256 + c * 128 + 128)
                        acc[b, rows, cols] = (
                            acc[b, rows, cols] * fades[t] + mixed[:, c * 128 : c * 128 + 128]
                        )

    def forward(step, sub):
        for direction in range(2):
            ring_copy(direction, step, sub).wait_recv()
            if step + 1 < RING_STEPS:
                ring_copy(direction, step + 1, sub).start()
        if step + 1 == RING_STEPS:
            last_copy(sub).start()
        for rel in (CLASSES - step - 1, step + 1):
            core_copy(rel, sub).start()

    def end(sub):
        last_copy(sub).wait_recv()
        core_copy(last, sub).start()

    def absorb():
        copies[2].wait()

        @pl.loop(1, N_HEAD)
        def _(i):
            q_copy(i).wait_recv()

        copies[3].wait()
        copies[4].wait()
        low = lax.broadcasted_iota(jnp.int32, (8 * N_HEAD, 128), 1) < 64
        for pair in range(HEADS // 2):
            tiles = []
            for t in range(3):
                column = pair * 384 + t * 128
                tiles.append(
                    jnp.concatenate(
                        [
                            q_land[:, h * HEAD_COLS + column : h * HEAD_COLS + column + 128].astype(
                                jnp.float32
                            )
                            for h in range(N_HEAD)
                        ],
                        axis=0,
                    )
                )
            swap1 = pltpu.roll(tiles[1], 64, 1)
            swap2 = pltpu.roll(tiles[2], 64, 1)
            nopes = (tiles[0], jnp.where(low, swap1, swap2))
            ropes = (jnp.where(low, tiles[1], swap1), jnp.where(low, swap2, tiles[2]))
            blank = jnp.zeros((128, 128), jnp.bfloat16)
            left = jnp.concatenate(
                [
                    jnp.concatenate([nopes[0].astype(jnp.bfloat16), blank], axis=1),
                    jnp.concatenate([blank, nopes[1].astype(jnp.bfloat16)], axis=1),
                ],
                axis=0,
            )
            for t in range(2):
                right = w_v[2 * pair : 2 * pair + 2, :, t * 256 : t * 256 + 256]
                pltpu.matmul_push_rhs(right.reshape(256, 256), 0, t)
                pltpu.matmul_acc_lhs(score_acc[2 * t + pair % 2], left, load_staged_rhs=0)
            for t in range(2):
                absorbed = pltpu.matmul_pop(score_acc[2 * t + pair % 2]).astype(jnp.bfloat16)
                for parity in range(2):
                    start = (2 * pair + parity) * 64
                    for b in range(2):
                        q_all[b, start : start + 64, t * 256 : t * 256 + 256] = absorbed[
                            parity * 128 + b * 64 : parity * 128 + b * 64 + 64
                        ]
            for parity in range(2):
                start = (2 * pair + parity) * 64
                rope = ropes[parity].astype(jnp.bfloat16)
                for b in range(2):
                    q_all[b, start : start + 64, KVL : KVL + 128] = rope[b * 64 : b * 64 + 64]

    take(0)
    for sub in range(SUBS):
        for direction in range(2):
            ring_copy(direction, 0, sub).start()
    share(0)
    give(2)
    absorb()
    attend((0, 0), (0, 1))
    forward(0, 0)
    attend((7, 0), (1, 0))
    forward(0, 1)
    take(1)
    share(4)
    attend((7, 1), (1, 1))
    forward(1, 0)
    attend((4, 0), (4, 1), (6, 0), (2, 0))
    forward(1, 1)
    take(2)
    share(direct(2))
    attend((6, 1), (2, 1))
    end(0)
    attend((direct(2), 0), (last, 0))
    end(1)
    attend((direct(2), 1), (last, 1))

    copies[5].wait()
    copies[6].wait()
    for pair in range(HEADS // 2):
        t = pair % 2
        rows = slice(pair * 128, pair * 128 + 128)
        for k in range(2):
            deep = slice(k * 256, k * 256 + 256)
            right = jnp.concatenate([v_v[2 * pair, deep, :], v_v[2 * pair + 1, deep, :]], axis=1)
            left = acc[:, rows, deep].reshape(256, 256).astype(jnp.bfloat16)
            pltpu.matmul_push_rhs(right, k, t)
            pltpu.matmul_acc_lhs(mix_acc[2 * t + pair // 2], left, load_staged_rhs=k)
    for pair in range(HEADS // 2):
        value = pltpu.matmul_pop(mix_acc[2 * (pair % 2) + pair // 2])
        sums = jnp.sum(
            total[:, pair * 128 : pair * 128 + 128, :].reshape(256, 128), axis=1, keepdims=True
        )
        for parity in range(2):
            parts = []
            for b in range(2):
                rows = slice(b * 128 + parity * 64, b * 128 + parity * 64 + 64)
                parts.append(value[rows, parity * 128 : parity * 128 + 128] / sums[rows])
            out_wide[pl.ds(2 * pair + parity, 128, stride=HEADS), :] = jnp.concatenate(
                parts, axis=0
            )
    out[...] = out_wide[...].astype(jnp.bfloat16).reshape(128, HEADS, VHD)

    @pl.loop(1, N_HEAD)
    def _(i):
        q_copy(i).wait_send()
        for d in range(nd):
            xy_copy(d, i).wait_send()

    for step in range(RING_STEPS):
        for sub in range(SUBS):
            for direction in range(2):
                ring_copy(direction, step, sub).wait_send()
    for sub in range(SUBS):
        last_copy(sub).wait_send()
        for rel in range(CLASSES):
            core_copy(rel, sub).wait_send()


def local(queries, cache_latent, cache_rope, selected, w_uk, value_up_weight):
    bf16 = jnp.bfloat16
    nd = len(DIRECT)
    dma = pltpu.SemaphoreType.DMA
    any_spec = pl.BlockSpec(memory_space=pl.ANY)
    return pl.pallas_call(
        kernel,
        out_shape=pltpu.VMEM((128, HEADS, VHD), bf16),
        in_specs=[any_spec] * 6,
        out_specs=pl.BlockSpec(memory_space=pltpu.VMEM),
        scratch_shapes=[
            pltpu.VMEM((32, 32), jnp.int32),
            pltpu.VMEM((32, 32), jnp.int32),
            pltpu.VMEM((40, 128), jnp.int32),
            pltpu.SMEM((40, 128), jnp.int32),
            pltpu.VMEM((128 * HEADS, VHD), jnp.float32),
            pltpu.VMEM((64, BLK, HALF), bf16),
            pltpu.VMEM((64, 2048), bf16),
            pltpu.VMEM((1024, 128), jnp.float32),
            pltpu.VMEM((64, 16, 128), bf16),
            pltpu.VMEM((4, SUB, BLK, 128), jnp.float32),
            pltpu.VMEM((HEADS, NOPE, KVL), bf16),
            pltpu.VMEM((HEADS, KVL, VHD), bf16),
            pltpu.VMEM((8, N_HEAD * HEAD_COLS), bf16),
            pltpu.VMEM((2, 512, KVL + 256), bf16),
            pltpu.VMEM((2, 512, KVL), jnp.float32),
            pltpu.VMEM((2, 512, 128), jnp.float32),
            pltpu.VMEM((2, 512, 128), jnp.float32),
            pltpu.VMEM((CLASSES, PICKS, SLOT, 128), bf16),
            pltpu.VMEM((CLASSES, PICKS, SLOT, 128), bf16),
        ]
        + [pltpu.VMEM((N_CTX, SLOT, 128), bf16)] * (2 * nd)
        + [
            dma((9,)),
            dma((N_HEAD,)),
            dma((N_HEAD,)),
            dma((nd, N_CTX)),
            dma((nd, N_CTX)),
            dma((2, RING_STEPS, SUBS)),
            dma((2, RING_STEPS, SUBS)),
            dma((SUBS,)),
            dma((SUBS,)),
            dma((CLASSES, SUBS)),
            dma((CLASSES, SUBS)),
        ],
        compiler_params=pltpu.CompilerParams(
            collective_id=0, has_side_effects=True, vmem_limit_bytes=62 * 1024 * 1024
        ),
    )(queries, cache_latent, cache_rope, selected, w_uk, value_up_weight)


def solution(mesh):
    placed = (
        P(("ctx", "head"), None),
        P("ctx", None, None),
        P("ctx", None),
        P(),
        P("head", None, None),
        P("head", None, None),
    )
    return jax.shard_map(
        local, mesh=mesh, in_specs=placed, out_specs=P("ctx", "head", None), check_vma=False
    )
```

```python
import functools
import math

import jax
import jax.numpy as jnp
from jax import lax
from jax.experimental import pallas as pl
from jax.experimental.pallas import tpu as pltpu
from jax.sharding import PartitionSpec as P

NOPE = 128
ROPE = 64
KVL = 512
VHD = 128
BLK = 64
HALF = KVL // 2
N_CTX = 16
N_HEAD = 16
HEADS = 8
HEAD_COLS = HEADS * (NOPE + ROPE)
SLOT = 144
CLASSES = 8
PICKS = 8
MESH = pl.DeviceIdType.MESH
DIRECT = (0, 4, 3)
RING_STEPS = 2
SUBS = 2
SUB = PICKS // SUBS
PIECE = 64
PIECES = 256 // PIECE
SCALE = math.log2(math.e) / math.sqrt(NOPE + ROPE)


def kernel(*refs):
    spaces = [
        pltpu.ACC(t)((PIECE, 256), jnp.float32) for t in (0, 0, 1, 1) for _ in range(PIECES)
    ] * 2
    pl.run_scoped(lambda *accumulators: body(accumulators, *refs), *spaces)


def body(
    accumulators,
    q_hbm,
    cache_hbm,
    rope_hbm,
    sel_hbm,
    w_hbm,
    v_hbm,
    out,
    sel_v,
    rank_v,
    tab_v,
    tab,
    out_wide,
    cache_v,
    rope_land,
    rope_wide,
    rope_v,
    rope_keys,
    w_v,
    v_v,
    q_land,
    q_all,
    acc,
    top,
    total,
    g_mine,
    g_other,
    *rest,
):
    nd = len(DIRECT)
    sets = [accumulators[i : i + PIECES] for i in range(0, 8 * PIECES, PIECES)]
    score_acc, mix_acc = sets[:4], sets[4:]

    def multiply(target, left, staged):
        for piece in range(PIECES):
            pltpu.matmul_acc_lhs(
                target[piece],
                left(piece * PIECE),
                load_staged_rhs=staged if piece == 0 else None,
            )

    def pop(target):
        return jnp.concatenate([pltpu.matmul_pop(piece) for piece in target], axis=0)

    send_bufs, recv_bufs = rest[:nd], rest[nd : 2 * nd]
    (
        local_sem,
        q_send,
        q_recv,
        xy_send,
        xy_recv,
        ring_send,
        ring_recv,
        last_send,
        last_recv,
        core_send,
        core_recv,
    ) = rest[2 * nd :]
    ctx = lax.axis_index("ctx")
    head = lax.axis_index("head")
    z = lax.div(head, 2)
    core = lax.rem(head, 2)

    def direct(d):
        return DIRECT[d] + 2 * core if d == 2 else DIRECT[d]

    def local_copies():
        mine = pl.multiple_of(core * HALF, HALF)
        other = pl.multiple_of(HALF - core * HALF, HALF)
        cols = pl.ds(pl.multiple_of(head * HEAD_COLS, 128), HEAD_COLS)
        return [
            pltpu.make_async_copy(
                cache_hbm.at[:, :, pl.ds(mine, HALF)], cache_v, local_sem.at[0]
            ),
            pltpu.make_async_copy(
                rope_hbm.at[:, pl.ds(pl.multiple_of(core * 2048, 2048), 2048)],
                rope_land,
                local_sem.at[1],
            ),
            pltpu.make_async_copy(q_hbm.at[:, cols], q_land.at[:, cols], local_sem.at[2]),
            pltpu.make_async_copy(
                w_hbm.at[:, :, pl.ds(mine, HALF)], w_v.at[:, :, pl.ds(0, HALF)], local_sem.at[3]
            ),
            pltpu.make_async_copy(
                w_hbm.at[:, :, pl.ds(other, HALF)],
                w_v.at[:, :, pl.ds(HALF, HALF)],
                local_sem.at[4],
            ),
            pltpu.make_async_copy(
                v_hbm.at[:, pl.ds(mine, HALF)], v_v.at[:, pl.ds(0, HALF)], local_sem.at[5]
            ),
            pltpu.make_async_copy(
                v_hbm.at[:, pl.ds(other, HALF)], v_v.at[:, pl.ds(HALF, HALF)], local_sem.at[6]
            ),
            pltpu.make_async_copy(sel_hbm, sel_v, local_sem.at[7]),
        ]

    copies = local_copies()
    for place in (7, 0, 1, 2, 3, 4, 5, 6):
        copies[place].start()

    barrier = pltpu.get_barrier_semaphore()

    @pl.loop(1, N_CTX)
    def _(i):
        pl.semaphore_signal(
            barrier,
            inc=1,
            device_id={"ctx": lax.rem(ctx + i, N_CTX), "head": head},
            device_id_type=MESH,
        )
        pl.semaphore_signal(
            barrier,
            inc=1,
            device_id={"ctx": ctx, "head": lax.rem(head + i, N_HEAD)},
            device_id_type=MESH,
        )

    copies[7].wait()
    sel = sel_v[...]
    rank = jnp.zeros_like(sel)
    for j in range(32):
        rank += (sel[:, j : j + 1] < sel).astype(jnp.int32)
    mine = lax.shift_right_logical(sel, 6) == ctx
    tab_v[...] = jnp.zeros_like(tab_v)
    for m in range(4):
        here = jnp.logical_and(mine, (rank & 3) == m)
        block = jnp.sum(jnp.where(here, sel & 63, 0), axis=1, keepdims=True)
        tab_v[0:32, m : m + 1] = block
    rank_v[...] = rank
    own_rank = rank_v[pl.ds(2 * ctx, 2), :]
    own_from = lax.shift_right_logical(sel_v[pl.ds(2 * ctx, 2), :], 6)
    position = lax.broadcasted_iota(jnp.int32, (2, 32), 1)
    source = jnp.zeros((2, 32), jnp.int32)
    for j in range(32):
        source += jnp.where(position == own_rank[:, j : j + 1], own_from[:, j : j + 1], 0)
    tab_v[32:34, 0:32] = source
    tab_copy = pltpu.make_async_copy(tab_v, tab, local_sem.at[8])
    tab_copy.start()

    def q_copy(i):
        to = 2 * lax.rem(z + 3 * i, 8) + lax.rem(core + lax.div(i, 8), 2)
        return pltpu.make_async_remote_copy(
            src_ref=q_hbm.at[:, pl.ds(pl.multiple_of(to * HEAD_COLS, 128), HEAD_COLS)],
            dst_ref=q_land.at[:, pl.ds(pl.multiple_of(head * HEAD_COLS, 128), HEAD_COLS)],
            send_sem=q_send.at[i],
            recv_sem=q_recv.at[i],
            device_id={"ctx": ctx, "head": to},
            device_id_type=MESH,
        )

    def partner(i):
        offset = lax.rem(7 * i, N_CTX)
        row = lax.rem(lax.div(ctx, 4) + lax.div(offset, 4), 4)
        return 4 * row + lax.rem(lax.rem(ctx, 4) + lax.rem(offset, 4), 4)

    def xy_copy(d, i):
        return pltpu.make_async_remote_copy(
            src_ref=send_bufs[d].at[i],
            dst_ref=recv_bufs[d].at[ctx],
            send_sem=xy_send.at[d, i],
            recv_sem=xy_recv.at[d, i],
            device_id={"ctx": partner(i), "head": head},
            device_id_type=MESH,
        )

    def picked(d, to):
        group = lax.rem(z + direct(d), CLASSES)
        block = tab[2 * to + lax.div(group, 4), lax.rem(group, 4)]
        return cache_v[block], rope_v[block]

    def stage(d):
        @pl.loop(1, N_CTX, unroll=5)
        def _(i):
            latent, rope = picked(d, partner(i))
            send_bufs[d][i, 0:64, :] = latent[:, :128]
            send_bufs[d][i, 64:128, :] = latent[:, 128:]
            send_bufs[d][i, 128:144, :] = rope

        latent, rope = picked(d, ctx)
        recv_bufs[d][ctx, 0:64, :] = latent[:, :128]
        recv_bufs[d][ctx, 64:128, :] = latent[:, 128:]
        recv_bufs[d][ctx, 128:144, :] = rope

    def give(d):
        @pl.loop(1, N_CTX, unroll=5)
        def _(i):
            xy_copy(d, i).start()

    pl.semaphore_wait(barrier, 2 * (N_CTX - 1))

    copies[1].wait()
    for i in range(16):
        rope_wide[pl.ds(i, 64, stride=16), :] = rope_land[:, i * 128 : i * 128 + 128].astype(
            jnp.float32
        )
    rope_v[...] = rope_wide[...].astype(jnp.bfloat16).reshape(64, 16, 128)
    copies[0].wait()
    tab_copy.wait()
    stage(0)
    give(0)

    @pl.loop(1, N_HEAD)
    def _(i):
        q_copy(i).start()

    for d in range(1, nd):
        stage(d)

    acc[...] = jnp.zeros_like(acc)
    total[...] = jnp.zeros_like(total)
    top[...] = jnp.full_like(top, -1e30)
    q_all[:, :, KVL + 128 :] = jnp.zeros((2, 512, 128), jnp.bfloat16)

    def ring_copy(direction, step, sub):
        source = (CLASSES - step) % CLASSES if direction == 0 else step
        target = CLASSES - step - 1 if direction == 0 else step + 1
        to = lax.rem(head + (2 if direction == 0 else N_HEAD - 2), N_HEAD)
        part = pl.ds(sub * SUB, SUB)
        return pltpu.make_async_remote_copy(
            src_ref=g_mine.at[source, part],
            dst_ref=g_mine.at[target, part],
            send_sem=ring_send.at[direction, step, sub],
            recv_sem=ring_recv.at[direction, step, sub],
            device_id={"ctx": ctx, "head": to},
            device_id_type=MESH,
        )

    last = 5 - 2 * core

    def last_copy(sub):
        part = pl.ds(sub * SUB, SUB)
        return pltpu.make_async_remote_copy(
            src_ref=g_mine.at[6 - 4 * core, part],
            dst_ref=g_mine.at[last, part],
            send_sem=last_send.at[sub],
            recv_sem=last_recv.at[sub],
            device_id={"ctx": ctx, "head": lax.rem(head + 2 + (N_HEAD - 4) * core, N_HEAD)},
            device_id_type=MESH,
        )

    def core_copy(rel, sub):
        part = pl.ds(sub * SUB, SUB)
        return pltpu.make_async_remote_copy(
            src_ref=g_mine.at[rel, part],
            dst_ref=g_other.at[rel, part],
            send_sem=core_send.at[rel, sub],
            recv_sem=core_recv.at[rel, sub],
            device_id={"ctx": ctx, "head": head + 1 - 2 * core},
            device_id_type=MESH,
        )

    def share(rel):
        for sub in range(SUBS):
            core_copy(rel, sub).start()

    def take(d):
        @pl.loop(1, 12)
        def _(i):
            xy_copy(d, i).wait_recv()

        if d == 0:
            give(1)

        @pl.loop(12, N_CTX)
        def _(i):
            xy_copy(d, i).wait_recv()

        rel = direct(d)
        group = lax.rem(z + rel, CLASSES)
        row = 32 + lax.div(group, 4)
        for j in range(PICKS):
            g_mine[rel, j] = recv_bufs[d][tab[row, lax.rem(group, 4) + 4 * j]]

    lane_low = lax.broadcasted_iota(jnp.int32, (SUB, 16, 128), 2) < 64
    blank = jnp.zeros((SUB * BLK, 128), jnp.bfloat16)

    def load(rel, sub, place):
        picks = pl.ds(sub * SUB, SUB)
        found = []
        for held, half in ((g_mine, core), (g_other, 1 - core)):
            found.append(
                jnp.concatenate(
                    [held[rel, picks, 0:64, :], held[rel, picks, 64:128, :]], axis=2
                ).reshape(SUB * BLK, HALF)
            )
            pairs = held[rel, picks, 128:144, :].astype(jnp.float32)
            zero = jnp.zeros_like(pairs)
            even = pl.ds(32 * half, 16, stride=2)
            odd = pl.ds(32 * half + 1, 16, stride=2)
            rope_keys[place, :, even, :] = jnp.where(lane_low, pairs, zero)
            rope_keys[place, :, odd, :] = jnp.where(lane_low, zero, pairs)
        rope = rope_keys[place].astype(jnp.bfloat16).reshape(SUB * BLK, 128)
        found.append(jnp.concatenate([rope, blank], axis=1))
        return found

    def attend(*items):
        for rel, sub in items:
            core_copy(rel, sub).wait_recv()
        groups = [lax.div(lax.rem(z + rel, CLASSES), 4) for rel, _ in items]
        loaded = [load(rel, sub, place) for place, (rel, sub) in enumerate(items)]

        def score(place):
            b = groups[place]
            for k in range(3):
                for t in range(2):
                    pltpu.matmul_push_rhs(loaded[place][k], k % 2, t, transpose=True)
                    multiply(
                        score_acc[2 * t + place % 2],
                        lambda first: q_all[
                            b,
                            t * 256 + first : t * 256 + first + PIECE,
                            k * 256 : k * 256 + 256,
                        ],
                        k % 2,
                    )

        score(0)
        for place, b in enumerate(groups):
            if place + 1 < len(items):
                score(place + 1)
            fades = []
            for t in range(2):
                weights = []
                for piece in range(PIECES):
                    rows = slice(t * 256 + piece * PIECE, t * 256 + piece * PIECE + PIECE)
                    scores = pltpu.matmul_pop(score_acc[2 * t + place % 2][piece])
                    before = top[b, rows, :]
                    now = jnp.maximum(before, jnp.max(scores, axis=1, keepdims=True))
                    fade = jnp.exp2((before - now) * SCALE)
                    parts = [
                        jnp.exp2((scores[:, c * 128 : c * 128 + 128] - now) * SCALE)
                        for c in range(2)
                    ]
                    top[b, rows, :] = now
                    total[b, rows, :] = total[b, rows, :] * fade + (parts[0] + parts[1])
                    weights.append(jnp.concatenate(parts, axis=1).astype(jnp.bfloat16))
                    fades.append(fade)
                for n in range(2):
                    pltpu.matmul_push_rhs(loaded[place][n], n, t)
                    multiply(mix_acc[2 * t + n], lambda first: weights[first // PIECE], n)
            for t in range(2):
                for piece in range(PIECES):
                    rows = slice(t * 256 + piece * PIECE, t * 256 + piece * PIECE + PIECE)
                    fade = fades[t * PIECES + piece]
                    for n in range(2):
                        mixed = pltpu.matmul_pop(mix_acc[2 * t + n][piece])
                        for c in range(2):
                            cols = slice(n * 256 + c * 128, n * 256 + c * 128 + 128)
                            acc[b, rows, cols] = (
                                acc[b, rows, cols] * fade + mixed[:, c * 128 : c * 128 + 128]
                            )

    def forward(step, sub):
        for direction in range(2):
            ring_copy(direction, step, sub).wait_recv()
            if step + 1 < RING_STEPS:
                ring_copy(direction, step + 1, sub).start()
        if step + 1 == RING_STEPS:
            last_copy(sub).start()
        for rel in (CLASSES - step - 1, step + 1):
            core_copy(rel, sub).start()

    def end(sub):
        last_copy(sub).wait_recv()
        core_copy(last, sub).start()

    def absorb():
        copies[2].wait()

        @pl.loop(1, N_HEAD)
        def _(i):
            q_copy(i).wait_recv()

        copies[3].wait()
        copies[4].wait()
        low = lax.broadcasted_iota(jnp.int32, (8 * N_HEAD, 128), 1) < 64
        for pair in range(HEADS // 2):
            tiles = []
            for t in range(3):
                column = pair * 384 + t * 128
                tiles.append(
                    jnp.concatenate(
                        [
                            q_land[:, h * HEAD_COLS + column : h * HEAD_COLS + column + 128].astype(
                                jnp.float32
                            )
                            for h in range(N_HEAD)
                        ],
                        axis=0,
                    )
                )
            swap1 = pltpu.roll(tiles[1], 64, 1)
            swap2 = pltpu.roll(tiles[2], 64, 1)
            nopes = (tiles[0], jnp.where(low, swap1, swap2))
            ropes = (jnp.where(low, tiles[1], swap1), jnp.where(low, swap2, tiles[2]))
            blank = jnp.zeros((128, 128), jnp.bfloat16)
            left = jnp.concatenate(
                [
                    jnp.concatenate([nopes[0].astype(jnp.bfloat16), blank], axis=1),
                    jnp.concatenate([blank, nopes[1].astype(jnp.bfloat16)], axis=1),
                ],
                axis=0,
            )
            for t in range(2):
                right = w_v[2 * pair : 2 * pair + 2, :, t * 256 : t * 256 + 256]
                pltpu.matmul_push_rhs(right.reshape(256, 256), 0, t)
                multiply(score_acc[2 * t + pair % 2], lambda first: left[first : first + PIECE], 0)
            for t in range(2):
                absorbed = pop(score_acc[2 * t + pair % 2]).astype(jnp.bfloat16)
                for parity in range(2):
                    start = (2 * pair + parity) * 64
                    for b in range(2):
                        q_all[b, start : start + 64, t * 256 : t * 256 + 256] = absorbed[
                            parity * 128 + b * 64 : parity * 128 + b * 64 + 64
                        ]
            for parity in range(2):
                start = (2 * pair + parity) * 64
                rope = ropes[parity].astype(jnp.bfloat16)
                for b in range(2):
                    q_all[b, start : start + 64, KVL : KVL + 128] = rope[b * 64 : b * 64 + 64]

    take(0)
    for sub in range(SUBS):
        for direction in range(2):
            ring_copy(direction, 0, sub).start()
    share(0)
    give(2)
    absorb()
    attend((0, 0), (0, 1))
    forward(0, 0)
    attend((7, 0), (1, 0))
    forward(0, 1)
    take(1)
    share(4)
    attend((7, 1), (1, 1))
    forward(1, 0)
    attend((4, 0), (4, 1), (6, 0), (2, 0))
    forward(1, 1)
    take(2)
    share(direct(2))
    attend((6, 1), (2, 1))
    end(0)
    attend((direct(2), 0), (last, 0))

    @pl.loop(1, N_HEAD)
    def _(i):
        q_copy(i).wait_send()
        for d in range(nd):
            xy_copy(d, i).wait_send()

    for step in range(RING_STEPS):
        for sub in range(SUBS):
            for direction in range(2):
                ring_copy(direction, step, sub).wait_send()
    last_copy(0).wait_send()
    core_copy(last, 0).wait_send()
    for rel in (0, 7, 1, 4, 6, 2, direct(2)):
        for sub in range(SUBS):
            core_copy(rel, sub).wait_send()
    end(1)
    attend((direct(2), 1), (last, 1))

    copies[5].wait()
    copies[6].wait()
    for pair in range(HEADS // 2):
        t = pair % 2
        rows = slice(pair * 128, pair * 128 + 128)
        for k in range(2):
            deep = slice(k * 256, k * 256 + 256)
            right = jnp.concatenate([v_v[2 * pair, deep, :], v_v[2 * pair + 1, deep, :]], axis=1)
            left = acc[:, rows, deep].reshape(256, 256).astype(jnp.bfloat16)
            pltpu.matmul_push_rhs(right, k, t)
            multiply(mix_acc[2 * t + pair // 2], lambda first: left[first : first + PIECE], k)
    for pair in range(HEADS // 2):
        value = pop(mix_acc[2 * (pair % 2) + pair // 2])
        sums = jnp.sum(
            total[:, pair * 128 : pair * 128 + 128, :].reshape(256, 128), axis=1, keepdims=True
        )
        for parity in range(2):
            parts = []
            for b in range(2):
                rows = slice(b * 128 + parity * 64, b * 128 + parity * 64 + 64)
                parts.append(value[rows, parity * 128 : parity * 128 + 128] / sums[rows])
            out_wide[pl.ds(2 * pair + parity, 128, stride=HEADS), :] = jnp.concatenate(
                parts, axis=0
            )
    out[...] = out_wide[...].astype(jnp.bfloat16).reshape(128, HEADS, VHD)

    last_copy(1).wait_send()
    core_copy(last, 1).wait_send()


def local(queries, cache_latent, cache_rope, selected, w_uk, value_up_weight):
    bf16 = jnp.bfloat16
    nd = len(DIRECT)
    dma = pltpu.SemaphoreType.DMA
    any_spec = pl.BlockSpec(memory_space=pl.ANY)
    return pl.pallas_call(
        kernel,
        out_shape=pltpu.VMEM((128, HEADS, VHD), bf16),
        in_specs=[any_spec] * 6,
        out_specs=pl.BlockSpec(memory_space=pltpu.VMEM),
        scratch_shapes=[
            pltpu.VMEM((32, 32), jnp.int32),
            pltpu.VMEM((32, 32), jnp.int32),
            pltpu.VMEM((40, 128), jnp.int32),
            pltpu.SMEM((40, 128), jnp.int32),
            pltpu.VMEM((128 * HEADS, VHD), jnp.float32),
            pltpu.VMEM((64, BLK, HALF), bf16),
            pltpu.VMEM((64, 2048), bf16),
            pltpu.VMEM((1024, 128), jnp.float32),
            pltpu.VMEM((64, 16, 128), bf16),
            pltpu.VMEM((4, SUB, BLK, 128), jnp.float32),
            pltpu.VMEM((HEADS, NOPE, KVL), bf16),
            pltpu.VMEM((HEADS, KVL, VHD), bf16),
            pltpu.VMEM((8, N_HEAD * HEAD_COLS), bf16),
            pltpu.VMEM((2, 512, KVL + 256), bf16),
            pltpu.VMEM((2, 512, KVL), jnp.float32),
            pltpu.VMEM((2, 512, 128), jnp.float32),
            pltpu.VMEM((2, 512, 128), jnp.float32),
            pltpu.VMEM((CLASSES, PICKS, SLOT, 128), bf16),
            pltpu.VMEM((CLASSES, PICKS, SLOT, 128), bf16),
        ]
        + [pltpu.VMEM((N_CTX, SLOT, 128), bf16)] * (2 * nd)
        + [
            dma((9,)),
            dma((N_HEAD,)),
            dma((N_HEAD,)),
            dma((nd, N_CTX)),
            dma((nd, N_CTX)),
            dma((2, RING_STEPS, SUBS)),
            dma((2, RING_STEPS, SUBS)),
            dma((SUBS,)),
            dma((SUBS,)),
            dma((CLASSES, SUBS)),
            dma((CLASSES, SUBS)),
        ],
        compiler_params=pltpu.CompilerParams(
            collective_id=0, has_side_effects=True, vmem_limit_bytes=62 * 1024 * 1024
        ),
    )(queries, cache_latent, cache_rope, selected, w_uk, value_up_weight)


def solution(mesh):
    placed = (
        P(("ctx", "head"), None),
        P("ctx", None, None),
        P("ctx", None),
        P(),
        P("head", None, None),
        P("head", None, None),
    )
    return jax.shard_map(
        local, mesh=mesh, in_specs=placed, out_specs=P("ctx", "head", None), check_vma=False
    )
```

```python
import functools
import math

import jax
import jax.numpy as jnp
from jax import lax
from jax.experimental import pallas as pl
from jax.experimental.pallas import tpu as pltpu
from jax.sharding import PartitionSpec as P

NOPE = 128
ROPE = 64
KVL = 512
VHD = 128
BLK = 64
HALF = KVL // 2
N_CTX = 16
N_HEAD = 16
HEADS = 8
HEAD_COLS = HEADS * (NOPE + ROPE)
SLOT = 144
SPLIT = 96
CLASSES = 8
PICKS = 8
MESH = pl.DeviceIdType.MESH
DIRECT = (0, 4, 3)
RING_STEPS = 2
SUBS = 2
SUB = PICKS // SUBS
PIECE = 64
PIECES = 256 // PIECE
SCALE = math.log2(math.e) / math.sqrt(NOPE + ROPE)


def kernel(*refs):
    spaces = [
        pltpu.ACC(t)((PIECE, 256), jnp.float32) for t in (0, 0, 1, 1) for _ in range(PIECES)
    ] * 2
    pl.run_scoped(lambda *accumulators: body(accumulators, *refs), *spaces)


def body(
    accumulators,
    q_hbm,
    cache_hbm,
    rope_hbm,
    sel_hbm,
    w_hbm,
    v_hbm,
    out,
    sel_v,
    rank_v,
    tab_v,
    tab,
    out_wide,
    cache_v,
    rope_land,
    rope_wide,
    rope_v,
    rope_keys,
    w_v,
    v_v,
    q_land,
    q_all,
    acc,
    top,
    total,
    g_mine,
    g_other,
    *rest,
):
    nd = len(DIRECT)
    sets = [accumulators[i : i + PIECES] for i in range(0, 8 * PIECES, PIECES)]
    score_acc, mix_acc = sets[:4], sets[4:]

    def multiply(target, left, staged):
        for piece in range(PIECES):
            pltpu.matmul_acc_lhs(
                target[piece],
                left(piece * PIECE),
                load_staged_rhs=staged if piece == 0 else None,
            )

    def pop(target):
        return jnp.concatenate([pltpu.matmul_pop(piece) for piece in target], axis=0)

    send_bufs, recv_bufs = rest[:nd], rest[nd : 2 * nd]
    (
        local_sem,
        q_send,
        q_recv,
        xy_send,
        xy_recv,
        ring_send,
        ring_recv,
        last_send,
        last_recv,
        rest_send,
        rest_recv,
        core_send,
        core_recv,
    ) = rest[2 * nd :]
    ctx = lax.axis_index("ctx")
    head = lax.axis_index("head")
    z = lax.div(head, 2)
    core = lax.rem(head, 2)

    def direct(d):
        return DIRECT[d] + 2 * core if d == 2 else DIRECT[d]

    def local_copies():
        mine = pl.multiple_of(core * HALF, HALF)
        other = pl.multiple_of(HALF - core * HALF, HALF)
        cols = pl.ds(pl.multiple_of(head * HEAD_COLS, 128), HEAD_COLS)
        return [
            pltpu.make_async_copy(
                cache_hbm.at[:, :, pl.ds(mine, HALF)], cache_v, local_sem.at[0]
            ),
            pltpu.make_async_copy(
                rope_hbm.at[:, pl.ds(pl.multiple_of(core * 2048, 2048), 2048)],
                rope_land,
                local_sem.at[1],
            ),
            pltpu.make_async_copy(q_hbm.at[:, cols], q_land.at[:, cols], local_sem.at[2]),
            pltpu.make_async_copy(
                w_hbm.at[:, :, pl.ds(mine, HALF)], w_v.at[:, :, pl.ds(0, HALF)], local_sem.at[3]
            ),
            pltpu.make_async_copy(
                w_hbm.at[:, :, pl.ds(other, HALF)],
                w_v.at[:, :, pl.ds(HALF, HALF)],
                local_sem.at[4],
            ),
            pltpu.make_async_copy(
                v_hbm.at[:, pl.ds(mine, HALF)], v_v.at[:, pl.ds(0, HALF)], local_sem.at[5]
            ),
            pltpu.make_async_copy(
                v_hbm.at[:, pl.ds(other, HALF)], v_v.at[:, pl.ds(HALF, HALF)], local_sem.at[6]
            ),
            pltpu.make_async_copy(sel_hbm, sel_v, local_sem.at[7]),
        ]

    copies = local_copies()
    for place in (7, 0, 1, 2, 3, 4, 5, 6):
        copies[place].start()

    barrier = pltpu.get_barrier_semaphore()

    @pl.loop(1, N_CTX)
    def _(i):
        pl.semaphore_signal(
            barrier,
            inc=1,
            device_id={"ctx": lax.rem(ctx + i, N_CTX), "head": head},
            device_id_type=MESH,
        )
        pl.semaphore_signal(
            barrier,
            inc=1,
            device_id={"ctx": ctx, "head": lax.rem(head + i, N_HEAD)},
            device_id_type=MESH,
        )

    copies[7].wait()
    sel = sel_v[...]
    rank = jnp.zeros_like(sel)
    for j in range(32):
        rank += (sel[:, j : j + 1] < sel).astype(jnp.int32)
    mine = lax.shift_right_logical(sel, 6) == ctx
    tab_v[...] = jnp.zeros_like(tab_v)
    for m in range(4):
        here = jnp.logical_and(mine, (rank & 3) == m)
        block = jnp.sum(jnp.where(here, sel & 63, 0), axis=1, keepdims=True)
        tab_v[0:32, m : m + 1] = block
    rank_v[...] = rank
    own_rank = rank_v[pl.ds(2 * ctx, 2), :]
    own_from = lax.shift_right_logical(sel_v[pl.ds(2 * ctx, 2), :], 6)
    position = lax.broadcasted_iota(jnp.int32, (2, 32), 1)
    source = jnp.zeros((2, 32), jnp.int32)
    for j in range(32):
        source += jnp.where(position == own_rank[:, j : j + 1], own_from[:, j : j + 1], 0)
    tab_v[32:34, 0:32] = source
    tab_copy = pltpu.make_async_copy(tab_v, tab, local_sem.at[8])
    tab_copy.start()

    def q_copy(i):
        to = 2 * lax.rem(z + 3 * i, 8) + lax.rem(core + lax.div(i, 8), 2)
        return pltpu.make_async_remote_copy(
            src_ref=q_hbm.at[:, pl.ds(pl.multiple_of(to * HEAD_COLS, 128), HEAD_COLS)],
            dst_ref=q_land.at[:, pl.ds(pl.multiple_of(head * HEAD_COLS, 128), HEAD_COLS)],
            send_sem=q_send.at[i],
            recv_sem=q_recv.at[i],
            device_id={"ctx": ctx, "head": to},
            device_id_type=MESH,
        )

    def partner(i):
        offset = lax.rem(7 * i, N_CTX)
        row = lax.rem(lax.div(ctx, 4) + lax.div(offset, 4), 4)
        return 4 * row + lax.rem(lax.rem(ctx, 4) + lax.rem(offset, 4), 4)

    def xy_copy(d, i):
        rows = pl.ds(0, SPLIT if d == 2 else SLOT)
        return pltpu.make_async_remote_copy(
            src_ref=send_bufs[d].at[i, rows],
            dst_ref=recv_bufs[d].at[ctx, rows],
            send_sem=xy_send.at[d, i],
            recv_sem=xy_recv.at[d, i],
            device_id={"ctx": partner(i), "head": head},
            device_id_type=MESH,
        )

    def picked(d, to):
        group = lax.rem(z + direct(d), CLASSES)
        block = tab[2 * to + lax.div(group, 4), lax.rem(group, 4)]
        return cache_v[block], rope_v[block]

    def stage(d):
        @pl.loop(1, N_CTX, unroll=5)
        def _(i):
            latent, rope = picked(d, partner(i))
            send_bufs[d][i, 0:64, :] = latent[:, :128]
            send_bufs[d][i, 64:128, :] = latent[:, 128:]
            send_bufs[d][i, 128:144, :] = rope

        latent, rope = picked(d, ctx)
        recv_bufs[d][ctx, 0:64, :] = latent[:, :128]
        recv_bufs[d][ctx, 64:128, :] = latent[:, 128:]
        recv_bufs[d][ctx, 128:144, :] = rope

    def give(d):
        @pl.loop(1, N_CTX, unroll=5)
        def _(i):
            xy_copy(d, i).start()

    pl.semaphore_wait(barrier, 2 * (N_CTX - 1))

    copies[1].wait()
    for i in range(16):
        rope_wide[pl.ds(i, 64, stride=16), :] = rope_land[:, i * 128 : i * 128 + 128].astype(
            jnp.float32
        )
    rope_v[...] = rope_wide[...].astype(jnp.bfloat16).reshape(64, 16, 128)
    copies[0].wait()
    tab_copy.wait()
    stage(0)
    give(0)

    @pl.loop(1, N_HEAD)
    def _(i):
        q_copy(i).start()

    for d in range(1, nd):
        stage(d)

    acc[...] = jnp.zeros_like(acc)
    total[...] = jnp.zeros_like(total)
    top[...] = jnp.full_like(top, -1e30)
    q_all[:, :, KVL + 128 :] = jnp.zeros((2, 512, 128), jnp.bfloat16)

    def ring_copy(direction, step, sub):
        source = (CLASSES - step) % CLASSES if direction == 0 else step
        target = CLASSES - step - 1 if direction == 0 else step + 1
        to = lax.rem(head + (2 if direction == 0 else N_HEAD - 2), N_HEAD)
        part = pl.ds(sub * SUB, SUB)
        return pltpu.make_async_remote_copy(
            src_ref=g_mine.at[source, part],
            dst_ref=g_mine.at[target, part],
            send_sem=ring_send.at[direction, step, sub],
            recv_sem=ring_recv.at[direction, step, sub],
            device_id={"ctx": ctx, "head": to},
            device_id_type=MESH,
        )

    last = 5 - 2 * core

    def last_copy(sub):
        part = pl.ds(sub * SUB, SUB)
        return pltpu.make_async_remote_copy(
            src_ref=g_mine.at[6 - 4 * core, part],
            dst_ref=g_mine.at[last, part],
            send_sem=last_send.at[sub],
            recv_sem=last_recv.at[sub],
            device_id={"ctx": ctx, "head": lax.rem(head + 2 + (N_HEAD - 4) * core, N_HEAD)},
            device_id_type=MESH,
        )

    def rest_copy(sub):
        part, rows = pl.ds(sub * SUB, SUB), pl.ds(SPLIT, SLOT - SPLIT)
        return pltpu.make_async_remote_copy(
            src_ref=g_mine.at[2 + 4 * core, part, rows],
            dst_ref=g_mine.at[direct(2), part, rows],
            send_sem=rest_send.at[sub],
            recv_sem=rest_recv.at[sub],
            device_id={"ctx": ctx, "head": lax.rem(head + 14 - (N_HEAD - 4) * core, N_HEAD)},
            device_id_type=MESH,
        )

    def core_copy(rel, sub):
        part = pl.ds(sub * SUB, SUB)
        return pltpu.make_async_remote_copy(
            src_ref=g_mine.at[rel, part],
            dst_ref=g_other.at[rel, part],
            send_sem=core_send.at[rel, sub],
            recv_sem=core_recv.at[rel, sub],
            device_id={"ctx": ctx, "head": head + 1 - 2 * core},
            device_id_type=MESH,
        )

    def share(rel):
        for sub in range(SUBS):
            core_copy(rel, sub).start()

    def take(d):
        @pl.loop(1, 12)
        def _(i):
            xy_copy(d, i).wait_recv()

        if d == 0:
            give(1)

        @pl.loop(12, N_CTX)
        def _(i):
            xy_copy(d, i).wait_recv()

        rel = direct(d)
        group = lax.rem(z + rel, CLASSES)
        row = 32 + lax.div(group, 4)
        for j in range(PICKS):
            source = tab[row, lax.rem(group, 4) + 4 * j]
            if d == 2:
                g_mine[rel, j, 0:SPLIT, :] = recv_bufs[d][source, 0:SPLIT, :]
            else:
                g_mine[rel, j] = recv_bufs[d][source]

    lane_low = lax.broadcasted_iota(jnp.int32, (SUB, 16, 128), 2) < 64
    blank = jnp.zeros((SUB * BLK, 128), jnp.bfloat16)

    def load(rel, sub, place):
        picks = pl.ds(sub * SUB, SUB)
        found = []
        for held, half in ((g_mine, core), (g_other, 1 - core)):
            found.append(
                jnp.concatenate(
                    [held[rel, picks, 0:64, :], held[rel, picks, 64:128, :]], axis=2
                ).reshape(SUB * BLK, HALF)
            )
            pairs = held[rel, picks, 128:144, :].astype(jnp.float32)
            zero = jnp.zeros_like(pairs)
            even = pl.ds(32 * half, 16, stride=2)
            odd = pl.ds(32 * half + 1, 16, stride=2)
            rope_keys[place, :, even, :] = jnp.where(lane_low, pairs, zero)
            rope_keys[place, :, odd, :] = jnp.where(lane_low, zero, pairs)
        rope = rope_keys[place].astype(jnp.bfloat16).reshape(SUB * BLK, 128)
        found.append(jnp.concatenate([rope, blank], axis=1))
        return found

    def attend(*items):
        for rel, sub in items:
            core_copy(rel, sub).wait_recv()
        groups = [lax.div(lax.rem(z + rel, CLASSES), 4) for rel, _ in items]
        loaded = [load(rel, sub, place) for place, (rel, sub) in enumerate(items)]

        def score(place):
            b = groups[place]
            for k in range(3):
                for t in range(2):
                    pltpu.matmul_push_rhs(loaded[place][k], k % 2, t, transpose=True)
                    multiply(
                        score_acc[2 * t + place % 2],
                        lambda first: q_all[
                            b,
                            t * 256 + first : t * 256 + first + PIECE,
                            k * 256 : k * 256 + 256,
                        ],
                        k % 2,
                    )

        score(0)
        for place, b in enumerate(groups):
            if place + 1 < len(items):
                score(place + 1)
            fades = []
            for t in range(2):
                weights = []
                for piece in range(PIECES):
                    rows = slice(t * 256 + piece * PIECE, t * 256 + piece * PIECE + PIECE)
                    scores = pltpu.matmul_pop(score_acc[2 * t + place % 2][piece])
                    before = top[b, rows, :]
                    now = jnp.maximum(before, jnp.max(scores, axis=1, keepdims=True))
                    fade = jnp.exp2((before - now) * SCALE)
                    parts = [
                        jnp.exp2((scores[:, c * 128 : c * 128 + 128] - now) * SCALE)
                        for c in range(2)
                    ]
                    top[b, rows, :] = now
                    total[b, rows, :] = total[b, rows, :] * fade + (parts[0] + parts[1])
                    weights.append(jnp.concatenate(parts, axis=1).astype(jnp.bfloat16))
                    fades.append(fade)
                for n in range(2):
                    pltpu.matmul_push_rhs(loaded[place][n], n, t)
                    multiply(mix_acc[2 * t + n], lambda first: weights[first // PIECE], n)
            for t in range(2):
                for piece in range(PIECES):
                    rows = slice(t * 256 + piece * PIECE, t * 256 + piece * PIECE + PIECE)
                    fade = fades[t * PIECES + piece]
                    for n in range(2):
                        mixed = pltpu.matmul_pop(mix_acc[2 * t + n][piece])
                        for c in range(2):
                            cols = slice(n * 256 + c * 128, n * 256 + c * 128 + 128)
                            acc[b, rows, cols] = (
                                acc[b, rows, cols] * fade + mixed[:, c * 128 : c * 128 + 128]
                            )

    def forward(step, sub):
        for direction in range(2):
            ring_copy(direction, step, sub).wait_recv()
            if step + 1 < RING_STEPS:
                ring_copy(direction, step + 1, sub).start()
        if step + 1 == RING_STEPS:
            last_copy(sub).start()
            rest_copy(sub).start()
        for rel in (CLASSES - step - 1, step + 1):
            core_copy(rel, sub).start()

    def end(sub):
        last_copy(sub).wait_recv()
        core_copy(last, sub).start()
        rest_copy(sub).wait_recv()
        core_copy(direct(2), sub).start()

    def absorb():
        copies[2].wait()

        @pl.loop(1, N_HEAD)
        def _(i):
            q_copy(i).wait_recv()

        copies[3].wait()
        copies[4].wait()
        low = lax.broadcasted_iota(jnp.int32, (8 * N_HEAD, 128), 1) < 64
        for pair in range(HEADS // 2):
            tiles = []
            for t in range(3):
                column = pair * 384 + t * 128
                tiles.append(
                    jnp.concatenate(
                        [
                            q_land[:, h * HEAD_COLS + column : h * HEAD_COLS + column + 128].astype(
                                jnp.float32
                            )
                            for h in range(N_HEAD)
                        ],
                        axis=0,
                    )
                )
            swap1 = pltpu.roll(tiles[1], 64, 1)
            swap2 = pltpu.roll(tiles[2], 64, 1)
            nopes = (tiles[0], jnp.where(low, swap1, swap2))
            ropes = (jnp.where(low, tiles[1], swap1), jnp.where(low, swap2, tiles[2]))
            blank = jnp.zeros((128, 128), jnp.bfloat16)
            left = jnp.concatenate(
                [
                    jnp.concatenate([nopes[0].astype(jnp.bfloat16), blank], axis=1),
                    jnp.concatenate([blank, nopes[1].astype(jnp.bfloat16)], axis=1),
                ],
                axis=0,
            )
            for t in range(2):
                right = w_v[2 * pair : 2 * pair + 2, :, t * 256 : t * 256 + 256]
                pltpu.matmul_push_rhs(right.reshape(256, 256), 0, t)
                multiply(score_acc[2 * t + pair % 2], lambda first: left[first : first + PIECE], 0)
            for t in range(2):
                absorbed = pop(score_acc[2 * t + pair % 2]).astype(jnp.bfloat16)
                for parity in range(2):
                    start = (2 * pair + parity) * 64
                    for b in range(2):
                        q_all[b, start : start + 64, t * 256 : t * 256 + 256] = absorbed[
                            parity * 128 + b * 64 : parity * 128 + b * 64 + 64
                        ]
            for parity in range(2):
                start = (2 * pair + parity) * 64
                rope = ropes[parity].astype(jnp.bfloat16)
                for b in range(2):
                    q_all[b, start : start + 64, KVL : KVL + 128] = rope[b * 64 : b * 64 + 64]

    take(0)
    for sub in range(SUBS):
        for direction in range(2):
            ring_copy(direction, 0, sub).start()
    share(0)
    give(2)
    absorb()
    attend((0, 0), (0, 1))
    forward(0, 0)
    attend((7, 0), (1, 0))
    forward(0, 1)
    attend((7, 1), (1, 1))
    forward(1, 0)
    take(1)
    share(4)
    attend((6, 0), (2, 0))
    forward(1, 1)
    attend((4, 0), (4, 1), (6, 1), (2, 1))
    take(2)
    end(0)
    attend((direct(2), 0), (last, 0))

    @pl.loop(1, N_HEAD)
    def _(i):
        q_copy(i).wait_send()
        for d in range(nd):
            xy_copy(d, i).wait_send()

    for step in range(RING_STEPS):
        for sub in range(SUBS):
            for direction in range(2):
                ring_copy(direction, step, sub).wait_send()
    last_copy(0).wait_send()
    rest_copy(0).wait_send()
    core_copy(last, 0).wait_send()
    core_copy(direct(2), 0).wait_send()
    for rel in (0, 7, 1, 4, 6, 2):
        for sub in range(SUBS):
            core_copy(rel, sub).wait_send()
    end(1)
    attend((direct(2), 1), (last, 1))

    copies[5].wait()
    copies[6].wait()
    for pair in range(HEADS // 2):
        t = pair % 2
        rows = slice(pair * 128, pair * 128 + 128)
        for k in range(2):
            deep = slice(k * 256, k * 256 + 256)
            right = jnp.concatenate([v_v[2 * pair, deep, :], v_v[2 * pair + 1, deep, :]], axis=1)
            left = acc[:, rows, deep].reshape(256, 256).astype(jnp.bfloat16)
            pltpu.matmul_push_rhs(right, k, t)
            multiply(mix_acc[2 * t + pair // 2], lambda first: left[first : first + PIECE], k)
    for pair in range(HEADS // 2):
        value = pop(mix_acc[2 * (pair % 2) + pair // 2])
        sums = jnp.sum(
            total[:, pair * 128 : pair * 128 + 128, :].reshape(256, 128), axis=1, keepdims=True
        )
        for parity in range(2):
            parts = []
            for b in range(2):
                rows = slice(b * 128 + parity * 64, b * 128 + parity * 64 + 64)
                parts.append(value[rows, parity * 128 : parity * 128 + 128] / sums[rows])
            out_wide[pl.ds(2 * pair + parity, 128, stride=HEADS), :] = jnp.concatenate(
                parts, axis=0
            )
    out[...] = out_wide[...].astype(jnp.bfloat16).reshape(128, HEADS, VHD)

    last_copy(1).wait_send()
    rest_copy(1).wait_send()
    core_copy(last, 1).wait_send()
    core_copy(direct(2), 1).wait_send()


def local(queries, cache_latent, cache_rope, selected, w_uk, value_up_weight):
    bf16 = jnp.bfloat16
    nd = len(DIRECT)
    dma = pltpu.SemaphoreType.DMA
    any_spec = pl.BlockSpec(memory_space=pl.ANY)
    return pl.pallas_call(
        kernel,
        out_shape=pltpu.VMEM((128, HEADS, VHD), bf16),
        in_specs=[any_spec] * 6,
        out_specs=pl.BlockSpec(memory_space=pltpu.VMEM),
        scratch_shapes=[
            pltpu.VMEM((32, 32), jnp.int32),
            pltpu.VMEM((32, 32), jnp.int32),
            pltpu.VMEM((40, 128), jnp.int32),
            pltpu.SMEM((40, 128), jnp.int32),
            pltpu.VMEM((128 * HEADS, VHD), jnp.float32),
            pltpu.VMEM((64, BLK, HALF), bf16),
            pltpu.VMEM((64, 2048), bf16),
            pltpu.VMEM((1024, 128), jnp.float32),
            pltpu.VMEM((64, 16, 128), bf16),
            pltpu.VMEM((4, SUB, BLK, 128), jnp.float32),
            pltpu.VMEM((HEADS, NOPE, KVL), bf16),
            pltpu.VMEM((HEADS, KVL, VHD), bf16),
            pltpu.VMEM((8, N_HEAD * HEAD_COLS), bf16),
            pltpu.VMEM((2, 512, KVL + 256), bf16),
            pltpu.VMEM((2, 512, KVL), jnp.float32),
            pltpu.VMEM((2, 512, 128), jnp.float32),
            pltpu.VMEM((2, 512, 128), jnp.float32),
            pltpu.VMEM((CLASSES, PICKS, SLOT, 128), bf16),
            pltpu.VMEM((CLASSES, PICKS, SLOT, 128), bf16),
        ]
        + [pltpu.VMEM((N_CTX, SLOT, 128), bf16)] * (2 * nd)
        + [
            dma((9,)),
            dma((N_HEAD,)),
            dma((N_HEAD,)),
            dma((nd, N_CTX)),
            dma((nd, N_CTX)),
            dma((2, RING_STEPS, SUBS)),
            dma((2, RING_STEPS, SUBS)),
            dma((SUBS,)),
            dma((SUBS,)),
            dma((SUBS,)),
            dma((SUBS,)),
            dma((CLASSES, SUBS)),
            dma((CLASSES, SUBS)),
        ],
        compiler_params=pltpu.CompilerParams(
            collective_id=0, has_side_effects=True, vmem_limit_bytes=62 * 1024 * 1024
        ),
    )(queries, cache_latent, cache_rope, selected, w_uk, value_up_weight)


def solution(mesh):
    placed = (
        P(("ctx", "head"), None),
        P("ctx", None, None),
        P("ctx", None),
        P(),
        P("head", None, None),
        P("head", None, None),
    )
    return jax.shard_map(
        local, mesh=mesh, in_specs=placed, out_specs=P("ctx", "head", None), check_vma=False
    )
```

```python
import functools
import math

import jax
import jax.numpy as jnp
from jax import lax
from jax.experimental import pallas as pl
from jax.experimental.pallas import tpu as pltpu
from jax.sharding import PartitionSpec as P

NOPE = 128
ROPE = 64
KVL = 512
VHD = 128
BLK = 64
HALF = KVL // 2
N_CTX = 16
N_HEAD = 16
HEADS = 8
HEAD_COLS = HEADS * (NOPE + ROPE)
SLOT = 144
CLASSES = 8
PICKS = 8
MESH = pl.DeviceIdType.MESH
DIRECT = (0, 4, 3)
RING_STEPS = 2
SUBS = 2
SUB = PICKS // SUBS
PIECE = 64
PIECES = 256 // PIECE
SCALE = math.log2(math.e) / math.sqrt(NOPE + ROPE)


def kernel(*refs):
    spaces = [
        pltpu.ACC(t)((PIECE, 256), jnp.float32) for t in (0, 0, 1, 1) for _ in range(PIECES)
    ] * 2
    pl.run_scoped(lambda *accumulators: body(accumulators, *refs), *spaces)


def body(
    accumulators,
    q_hbm,
    cache_hbm,
    rope_hbm,
    sel_hbm,
    w_hbm,
    v_hbm,
    out,
    sel_v,
    rank_v,
    tab_v,
    tab,
    out_wide,
    cache_v,
    rope_land,
    rope_wide,
    rope_v,
    rope_keys,
    w_v,
    v_v,
    q_land,
    q_all,
    acc,
    top,
    total,
    g_mine,
    g_other,
    *rest,
):
    nd = len(DIRECT)
    sets = [accumulators[i : i + PIECES] for i in range(0, 8 * PIECES, PIECES)]
    score_acc, mix_acc = sets[:4], sets[4:]

    def multiply(target, left, staged):
        for piece in range(PIECES):
            pltpu.matmul_acc_lhs(
                target[piece],
                left(piece * PIECE),
                load_staged_rhs=staged if piece == 0 else None,
            )

    def pop(target):
        return jnp.concatenate([pltpu.matmul_pop(piece) for piece in target], axis=0)

    send_bufs, recv_bufs = rest[:nd], rest[nd : 2 * nd]
    (
        local_sem,
        q_send,
        q_recv,
        xy_send,
        xy_recv,
        ring_send,
        ring_recv,
        last_send,
        last_recv,
        core_send,
        core_recv,
    ) = rest[2 * nd :]
    ctx = lax.axis_index("ctx")
    head = lax.axis_index("head")
    z = lax.div(head, 2)
    core = lax.rem(head, 2)

    def direct(d):
        return DIRECT[d] + 2 * core if d == 2 else DIRECT[d]

    def local_copies():
        mine = pl.multiple_of(core * HALF, HALF)
        other = pl.multiple_of(HALF - core * HALF, HALF)
        cols = pl.ds(pl.multiple_of(head * HEAD_COLS, 128), HEAD_COLS)
        return [
            pltpu.make_async_copy(
                cache_hbm.at[:, :, pl.ds(mine, HALF)], cache_v, local_sem.at[0]
            ),
            pltpu.make_async_copy(
                rope_hbm.at[:, pl.ds(pl.multiple_of(core * 2048, 2048), 2048)],
                rope_land,
                local_sem.at[1],
            ),
            pltpu.make_async_copy(q_hbm.at[:, cols], q_land.at[:, cols], local_sem.at[2]),
            pltpu.make_async_copy(
                w_hbm.at[:, :, pl.ds(mine, HALF)], w_v.at[:, :, pl.ds(0, HALF)], local_sem.at[3]
            ),
            pltpu.make_async_copy(
                w_hbm.at[:, :, pl.ds(other, HALF)],
                w_v.at[:, :, pl.ds(HALF, HALF)],
                local_sem.at[4],
            ),
            pltpu.make_async_copy(
                v_hbm.at[:, pl.ds(mine, HALF)], v_v.at[:, pl.ds(0, HALF)], local_sem.at[5]
            ),
            pltpu.make_async_copy(
                v_hbm.at[:, pl.ds(other, HALF)], v_v.at[:, pl.ds(HALF, HALF)], local_sem.at[6]
            ),
            pltpu.make_async_copy(sel_hbm, sel_v, local_sem.at[7]),
        ]

    copies = local_copies()
    for place in (7, 0, 1):
        copies[place].start()

    barrier = pltpu.get_barrier_semaphore()

    @pl.loop(1, N_CTX)
    def _(i):
        pl.semaphore_signal(
            barrier,
            inc=1,
            device_id={"ctx": lax.rem(ctx + i, N_CTX), "head": head},
            device_id_type=MESH,
        )
        pl.semaphore_signal(
            barrier,
            inc=1,
            device_id={"ctx": ctx, "head": lax.rem(head + i, N_HEAD)},
            device_id_type=MESH,
        )

    for place in (2, 3, 4, 5, 6):
        copies[place].start()

    copies[7].wait()
    sel = sel_v[...]
    rank = jnp.zeros_like(sel)
    for j in range(32):
        rank += (sel[:, j : j + 1] < sel).astype(jnp.int32)
    mine = lax.shift_right_logical(sel, 6) == ctx
    tab_v[...] = jnp.zeros_like(tab_v)
    for m in range(4):
        here = jnp.logical_and(mine, (rank & 3) == m)
        block = jnp.sum(jnp.where(here, sel & 63, 0), axis=1, keepdims=True)
        tab_v[0:32, m : m + 1] = block
    rank_v[...] = rank
    own_rank = rank_v[pl.ds(2 * ctx, 2), :]
    own_from = lax.shift_right_logical(sel_v[pl.ds(2 * ctx, 2), :], 6)
    position = lax.broadcasted_iota(jnp.int32, (2, 32), 1)
    source = jnp.zeros((2, 32), jnp.int32)
    for j in range(32):
        source += jnp.where(position == own_rank[:, j : j + 1], own_from[:, j : j + 1], 0)
    tab_v[32:34, 0:32] = source
    tab_copy = pltpu.make_async_copy(tab_v, tab, local_sem.at[8])
    tab_copy.start()

    def q_copy(i):
        to = 2 * lax.rem(z + 3 * i, 8) + lax.rem(core + lax.div(i, 8), 2)
        return pltpu.make_async_remote_copy(
            src_ref=q_hbm.at[:, pl.ds(pl.multiple_of(to * HEAD_COLS, 128), HEAD_COLS)],
            dst_ref=q_land.at[:, pl.ds(pl.multiple_of(head * HEAD_COLS, 128), HEAD_COLS)],
            send_sem=q_send.at[i],
            recv_sem=q_recv.at[i],
            device_id={"ctx": ctx, "head": to},
            device_id_type=MESH,
        )

    def partner(i):
        offset = lax.rem(7 * i, N_CTX)
        row = lax.rem(lax.div(ctx, 4) + lax.div(offset, 4), 4)
        return 4 * row + lax.rem(lax.rem(ctx, 4) + lax.rem(offset, 4), 4)

    def xy_copy(d, i):
        return pltpu.make_async_remote_copy(
            src_ref=send_bufs[d].at[i],
            dst_ref=recv_bufs[d].at[ctx],
            send_sem=xy_send.at[d, i],
            recv_sem=xy_recv.at[d, i],
            device_id={"ctx": partner(i), "head": head},
            device_id_type=MESH,
        )

    def picked(d, to):
        group = lax.rem(z + direct(d), CLASSES)
        block = tab[2 * to + lax.div(group, 4), lax.rem(group, 4)]
        return cache_v[block], rope_v[block]

    def stage(d):
        @pl.loop(1, N_CTX, unroll=5)
        def _(i):
            latent, rope = picked(d, partner(i))
            send_bufs[d][i, 0:64, :] = latent[:, :128]
            send_bufs[d][i, 64:128, :] = latent[:, 128:]
            send_bufs[d][i, 128:144, :] = rope

        latent, rope = picked(d, ctx)
        recv_bufs[d][ctx, 0:64, :] = latent[:, :128]
        recv_bufs[d][ctx, 64:128, :] = latent[:, 128:]
        recv_bufs[d][ctx, 128:144, :] = rope

    def give(d):
        @pl.loop(1, N_CTX, unroll=5)
        def _(i):
            xy_copy(d, i).start()

    pl.semaphore_wait(barrier, 2 * (N_CTX - 1))

    copies[1].wait()
    for i in range(16):
        rope_wide[pl.ds(i, 64, stride=16), :] = rope_land[:, i * 128 : i * 128 + 128].astype(
            jnp.float32
        )
    rope_v[...] = rope_wide[0:1024, :].astype(jnp.bfloat16).reshape(64, 16, 128)
    copies[0].wait()
    tab_copy.wait()
    stage(0)
    give(0)

    @pl.loop(1, N_HEAD)
    def _(i):
        q_copy(i).start()

    for d in range(1, nd):
        stage(d)

    acc[...] = jnp.zeros_like(acc)
    total[...] = jnp.zeros_like(total)
    top[...] = jnp.full_like(top, -1e30)
    q_all[:, :, KVL + 128 :] = jnp.zeros((2, 512, 128), jnp.bfloat16)

    def ring_copy(direction, step, sub):
        source = (CLASSES - step) % CLASSES if direction == 0 else step
        target = CLASSES - step - 1 if direction == 0 else step + 1
        to = lax.rem(head + (2 if direction == 0 else N_HEAD - 2), N_HEAD)
        part = pl.ds(sub * SUB, SUB)
        return pltpu.make_async_remote_copy(
            src_ref=g_mine.at[source, part],
            dst_ref=g_mine.at[target, part],
            send_sem=ring_send.at[direction, step, sub],
            recv_sem=ring_recv.at[direction, step, sub],
            device_id={"ctx": ctx, "head": to},
            device_id_type=MESH,
        )

    last = 5 - 2 * core

    def last_copy(sub):
        part = pl.ds(sub * SUB, SUB)
        return pltpu.make_async_remote_copy(
            src_ref=g_mine.at[6 - 4 * core, part],
            dst_ref=g_mine.at[last, part],
            send_sem=last_send.at[sub],
            recv_sem=last_recv.at[sub],
            device_id={"ctx": ctx, "head": lax.rem(head + 2 + (N_HEAD - 4) * core, N_HEAD)},
            device_id_type=MESH,
        )

    def core_copy(rel, sub):
        part = pl.ds(sub * SUB, SUB)
        return pltpu.make_async_remote_copy(
            src_ref=g_mine.at[rel, part],
            dst_ref=g_other.at[rel, part],
            send_sem=core_send.at[rel, sub],
            recv_sem=core_recv.at[rel, sub],
            device_id={"ctx": ctx, "head": head + 1 - 2 * core},
            device_id_type=MESH,
        )

    def share(rel):
        for sub in range(SUBS):
            core_copy(rel, sub).start()

    def take(d):
        @pl.loop(1, 12)
        def _(i):
            xy_copy(d, i).wait_recv()

        if d == 0:
            give(1)

        @pl.loop(12, N_CTX)
        def _(i):
            xy_copy(d, i).wait_recv()

        rel = direct(d)
        group = lax.rem(z + rel, CLASSES)
        row = 32 + lax.div(group, 4)
        for j in range(PICKS):
            g_mine[rel, j] = recv_bufs[d][tab[row, lax.rem(group, 4) + 4 * j]]

    lane_low = lax.broadcasted_iota(jnp.int32, (SUB, 16, 128), 2) < 64
    blank = jnp.zeros((SUB * BLK, 128), jnp.bfloat16)

    def load(rel, sub, place):
        picks = pl.ds(sub * SUB, SUB)
        found = []
        for held, half in ((g_mine, core), (g_other, 1 - core)):
            found.append(
                jnp.concatenate(
                    [held[rel, picks, 0:64, :], held[rel, picks, 64:128, :]], axis=2
                ).reshape(SUB * BLK, HALF)
            )
            pairs = held[rel, picks, 128:144, :].astype(jnp.float32)
            zero = jnp.zeros_like(pairs)
            even = pl.ds(32 * half, 16, stride=2)
            odd = pl.ds(32 * half + 1, 16, stride=2)
            rope_keys[place, :, even, :] = jnp.where(lane_low, pairs, zero)
            rope_keys[place, :, odd, :] = jnp.where(lane_low, zero, pairs)
        rope = rope_keys[place, :, 0:BLK, :].astype(jnp.bfloat16).reshape(SUB * BLK, 128)
        found.append(jnp.concatenate([rope, blank], axis=1))
        return found

    def attend(*items):
        for rel, sub in items:
            core_copy(rel, sub).wait_recv()
        groups = [lax.div(lax.rem(z + rel, CLASSES), 4) for rel, _ in items]
        loaded = [load(rel, sub, place) for place, (rel, sub) in enumerate(items)]

        def score(place):
            b = groups[place]
            for k in range(3):
                for t in range(2):
                    pltpu.matmul_push_rhs(loaded[place][k], k % 2, t, transpose=True)
                    multiply(
                        score_acc[2 * t + place % 2],
                        lambda first: q_all[
                            b,
                            t * 256 + first : t * 256 + first + PIECE,
                            k * 256 : k * 256 + 256,
                        ],
                        k % 2,
                    )

        score(0)
        for place, b in enumerate(groups):
            if place + 1 < len(items):
                score(place + 1)
            fades = []
            for t in range(2):
                weights = []
                for piece in range(PIECES):
                    rows = slice(t * 256 + piece * PIECE, t * 256 + piece * PIECE + PIECE)
                    scores = pltpu.matmul_pop(score_acc[2 * t + place % 2][piece])
                    before = top[b, rows, :]
                    now = jnp.maximum(before, jnp.max(scores, axis=1, keepdims=True))
                    fade = jnp.exp2((before - now) * SCALE)
                    parts = [
                        jnp.exp2((scores[:, c * 128 : c * 128 + 128] - now) * SCALE)
                        for c in range(2)
                    ]
                    top[b, rows, :] = now
                    total[b, rows, :] = total[b, rows, :] * fade + (parts[0] + parts[1])
                    weights.append(jnp.concatenate(parts, axis=1).astype(jnp.bfloat16))
                    fades.append(fade)
                for n in range(2):
                    pltpu.matmul_push_rhs(loaded[place][n], n, t)
                    multiply(mix_acc[2 * t + n], lambda first: weights[first // PIECE], n)
            for t in range(2):
                for piece in range(PIECES):
                    rows = slice(t * 256 + piece * PIECE, t * 256 + piece * PIECE + PIECE)
                    fade = fades[t * PIECES + piece]
                    for n in range(2):
                        mixed = pltpu.matmul_pop(mix_acc[2 * t + n][piece])
                        for c in range(2):
                            cols = slice(n * 256 + c * 128, n * 256 + c * 128 + 128)
                            acc[b, rows, cols] = (
                                acc[b, rows, cols] * fade + mixed[:, c * 128 : c * 128 + 128]
                            )

    def forward(step, sub):
        for direction in range(2):
            ring_copy(direction, step, sub).wait_recv()
            if step + 1 < RING_STEPS:
                ring_copy(direction, step + 1, sub).start()
        if step + 1 == RING_STEPS:
            last_copy(sub).start()
        for rel in (CLASSES - step - 1, step + 1):
            core_copy(rel, sub).start()

    def end(sub):
        last_copy(sub).wait_recv()
        core_copy(last, sub).start()

    def absorb():
        copies[2].wait()

        @pl.loop(1, N_HEAD)
        def _(i):
            q_copy(i).wait_recv()

        copies[3].wait()
        copies[4].wait()
        low = lax.broadcasted_iota(jnp.int32, (8 * N_HEAD, 128), 1) < 64
        for pair in range(HEADS // 2):
            tiles = []
            for t in range(3):
                column = pair * 384 + t * 128
                tiles.append(
                    jnp.concatenate(
                        [
                            q_land[:, h * HEAD_COLS + column : h * HEAD_COLS + column + 128].astype(
                                jnp.float32
                            )
                            for h in range(N_HEAD)
                        ],
                        axis=0,
                    )
                )
            swap1 = pltpu.roll(tiles[1], 64, 1)
            swap2 = pltpu.roll(tiles[2], 64, 1)
            nopes = (tiles[0], jnp.where(low, swap1, swap2))
            ropes = (jnp.where(low, tiles[1], swap1), jnp.where(low, swap2, tiles[2]))
            blank = jnp.zeros((128, 128), jnp.bfloat16)
            left = jnp.concatenate(
                [
                    jnp.concatenate([nopes[0].astype(jnp.bfloat16), blank], axis=1),
                    jnp.concatenate([blank, nopes[1].astype(jnp.bfloat16)], axis=1),
                ],
                axis=0,
            )
            for t in range(2):
                right = w_v[2 * pair : 2 * pair + 2, :, t * 256 : t * 256 + 256]
                pltpu.matmul_push_rhs(right.reshape(256, 256), 0, t)
                multiply(score_acc[2 * t + pair % 2], lambda first: left[first : first + PIECE], 0)
            for t in range(2):
                absorbed = pop(score_acc[2 * t + pair % 2]).astype(jnp.bfloat16)
                for parity in range(2):
                    start = (2 * pair + parity) * 64
                    for b in range(2):
                        q_all[b, start : start + 64, t * 256 : t * 256 + 256] = absorbed[
                            parity * 128 + b * 64 : parity * 128 + b * 64 + 64
                        ]
            for parity in range(2):
                start = (2 * pair + parity) * 64
                rope = ropes[parity].astype(jnp.bfloat16)
                for b in range(2):
                    q_all[b, start : start + 64, KVL : KVL + 128] = rope[b * 64 : b * 64 + 64]

    take(0)
    for sub in range(SUBS):
        for direction in range(2):
            ring_copy(direction, 0, sub).start()
    share(0)
    give(2)
    absorb()
    attend((0, 0), (0, 1))
    forward(0, 0)
    attend((7, 0), (1, 0))
    forward(0, 1)
    take(1)
    share(4)
    attend((7, 1), (1, 1))
    forward(1, 0)
    attend((4, 0), (4, 1), (6, 0), (2, 0))
    forward(1, 1)
    take(2)
    share(direct(2))
    attend((6, 1), (2, 1))
    end(0)
    attend((direct(2), 0), (last, 0))

    @pl.loop(1, N_HEAD)
    def _(i):
        q_copy(i).wait_send()
        for d in range(nd):
            xy_copy(d, i).wait_send()

    for step in range(RING_STEPS):
        for sub in range(SUBS):
            for direction in range(2):
                ring_copy(direction, step, sub).wait_send()
    last_copy(0).wait_send()
    core_copy(last, 0).wait_send()
    for rel in (0, 7, 1, 4, 6, 2, direct(2)):
        for sub in range(SUBS):
            core_copy(rel, sub).wait_send()
    end(1)
    attend((direct(2), 1), (last, 1))

    copies[5].wait()
    copies[6].wait()
    for pair in range(HEADS // 2):
        t = pair % 2
        rows = slice(pair * 128, pair * 128 + 128)
        for k in range(2):
            deep = slice(k * 256, k * 256 + 256)
            right = jnp.concatenate([v_v[2 * pair, deep, :], v_v[2 * pair + 1, deep, :]], axis=1)
            left = acc[:, rows, deep].reshape(256, 256).astype(jnp.bfloat16)
            pltpu.matmul_push_rhs(right, k, t)
            multiply(mix_acc[2 * t + pair // 2], lambda first: left[first : first + PIECE], k)
    for pair in range(HEADS // 2):
        value = pop(mix_acc[2 * (pair % 2) + pair // 2])
        sums = jnp.sum(
            total[:, pair * 128 : pair * 128 + 128, :].reshape(256, 128), axis=1, keepdims=True
        )
        for parity in range(2):
            parts = []
            for b in range(2):
                rows = slice(b * 128 + parity * 64, b * 128 + parity * 64 + 64)
                parts.append(value[rows, parity * 128 : parity * 128 + 128] / sums[rows])
            out_wide[pl.ds(2 * pair + parity, 128, stride=HEADS), :] = jnp.concatenate(
                parts, axis=0
            )
    out[...] = out_wide[0 : 128 * HEADS, :].astype(jnp.bfloat16).reshape(128, HEADS, VHD)

    last_copy(1).wait_send()
    core_copy(last, 1).wait_send()


def local(queries, cache_latent, cache_rope, selected, w_uk, value_up_weight):
    bf16 = jnp.bfloat16
    nd = len(DIRECT)
    dma = pltpu.SemaphoreType.DMA
    any_spec = pl.BlockSpec(memory_space=pl.ANY)
    return pl.pallas_call(
        kernel,
        out_shape=pltpu.VMEM((128, HEADS, VHD), bf16),
        in_specs=[any_spec] * 6,
        out_specs=pl.BlockSpec(memory_space=pltpu.VMEM),
        scratch_shapes=[
            pltpu.VMEM((32, 32), jnp.int32),
            pltpu.VMEM((32, 32), jnp.int32),
            pltpu.VMEM((40, 128), jnp.int32),
            pltpu.SMEM((40, 128), jnp.int32),
            pltpu.VMEM((128 * HEADS + HEADS, VHD), jnp.float32),
            pltpu.VMEM((64, BLK, HALF), bf16),
            pltpu.VMEM((64, 2048), bf16),
            pltpu.VMEM((1024 + 16, 128), jnp.float32),
            pltpu.VMEM((64, 16, 128), bf16),
            pltpu.VMEM((4, SUB, BLK + 8, 128), jnp.float32),
            pltpu.VMEM((HEADS, NOPE, KVL), bf16),
            pltpu.VMEM((HEADS, KVL, VHD), bf16),
            pltpu.VMEM((8, N_HEAD * HEAD_COLS), bf16),
            pltpu.VMEM((2, 512, KVL + 256), bf16),
            pltpu.VMEM((2, 512, KVL), jnp.float32),
            pltpu.VMEM((2, 512, 128), jnp.float32),
            pltpu.VMEM((2, 512, 128), jnp.float32),
            pltpu.VMEM((CLASSES, PICKS, SLOT, 128), bf16),
            pltpu.VMEM((CLASSES, PICKS, SLOT, 128), bf16),
        ]
        + [pltpu.VMEM((N_CTX, SLOT, 128), bf16)] * (2 * nd)
        + [
            dma((9,)),
            dma((N_HEAD,)),
            dma((N_HEAD,)),
            dma((nd, N_CTX)),
            dma((nd, N_CTX)),
            dma((2, RING_STEPS, SUBS)),
            dma((2, RING_STEPS, SUBS)),
            dma((SUBS,)),
            dma((SUBS,)),
            dma((CLASSES, SUBS)),
            dma((CLASSES, SUBS)),
        ],
        compiler_params=pltpu.CompilerParams(
            collective_id=0, has_side_effects=True, vmem_limit_bytes=62 * 1024 * 1024
        ),
    )(queries, cache_latent, cache_rope, selected, w_uk, value_up_weight)


def solution(mesh):
    placed = (
        P(("ctx", "head"), None),
        P("ctx", None, None),
        P("ctx", None),
        P(),
        P("head", None, None),
        P("head", None, None),
    )
    return jax.shard_map(
        local, mesh=mesh, in_specs=placed, out_specs=P("ctx", "head", None), check_vma=False
    )
```
